128 devices in a mesh: row: 8 (over x_lo, z), col: 16 (over x_hi, y, core).
Axes of the slice: x: 4 (x_hi: 2, x_lo: 2; x = x_hi * 2 + x_lo), y: 4, z: 4, core: 2. Of those that a mesh axis runs over, the one named last changes fastest.
Arguments:
- front: float32 [16384, 16384], P('row', 'col'), may hold values from -6 to 6
- inverses: float32 [2, 512, 512], replicated, may hold values from -2 to 2, as said below
- block_owner: int32 [128, 128], P('row', 'col'), may hold values from -1 to 127, as said below
- block_slot: int32 [128, 128], P('row', 'col'), may hold values from 0 to 47
- parent_in: float32 [6144, 128, 128], P(('row', 'col')), may hold values from -6 to 6
Outputs:
- updated: float32 [16384, 16384], P('row', 'col')
- panels: float32 [16384, 1024], P(('row', 'col'))
- parent_out: float32 [6144, 128, 128], P(('row', 'col'))
The draws below stay inside these ranges and needn't reach their ends.
Inputs may be any that keep to these rules, and one draw needn't show every extreme that they name: Entries of the pivot block inverses. `block_owner`: -1 exactly for blocks above the diagonal (I < J); on one device's 16 x 8 blocks no device is named more than 1 times, and on some device some device is named exactly 1 times.
All inputs are finite; a program needn't handle non-finite values.
Results may differ from the reference program's by a relative error of at most 0.00014.
Values sent between devices are 32-bit elements; how exact they have to be, the bound alone decides.
No kernel may reach another device: no remote copies, remote signals or barrier semaphores. Data moves between devices by JAX's collectives and lax.ppermute only.
A program may use at most 128 MiB of HBM per device.

```python
import jax
import jax.numpy as jnp
from jax import lax

PW = 512
BS = 128
PSLOT = 48
F = 16384
NB = 128
TRB = 16
TCB = 8
NROWS = 8
NCOLS = 16
NDEV = 128
PB = 6144


def draw_inverses(key, part):
    key_diag, key_noise = jax.random.split(jax.random.fold_in(key, 11))
    diagonal = jax.random.uniform(key_diag, (2, PW), jnp.float32, 1.0, 2.0)
    noise = jax.random.normal(key_noise, (2, PW, PW), jnp.float32)
    symmetric = (noise + jnp.transpose(noise, (0, 2, 1))) * (0.6 / (PW * 1.4142135))
    identity = jnp.eye(PW, dtype=jnp.float32)
    return symmetric * (1.0 - identity) + identity * (diagonal[:, :, None] / jnp.sqrt(jnp.float32(PW)))


def draw_block_owner(key, part):
    candidates = jax.random.permutation(jax.random.fold_in(key, 5), NDEV).astype(jnp.int32)
    position = jnp.arange(NDEV, dtype=jnp.int32)
    sort_keys = jnp.where(candidates == 1, -2, jnp.where(candidates == NDEV // 2, -1, position)).astype(jnp.int32)
    offsets = candidates[jnp.argsort(sort_keys, stable=True)].astype(jnp.int32)
    index = jnp.arange(NB, dtype=jnp.int32)
    block_row = index[:, None] + jnp.zeros((NB, NB), jnp.int32)
    block_col = index[None, :] + jnp.zeros((NB, NB), jnp.int32)
    lower = (block_row >= block_col).astype(jnp.int32)
    tiles = lower.reshape(NROWS, TRB, NCOLS, TCB).transpose(0, 2, 1, 3).reshape(NROWS, NCOLS, TRB * TCB)
    ranks = jnp.cumsum(tiles, axis=2) - tiles
    ranks = ranks.reshape(NROWS, NCOLS, TRB, TCB).transpose(0, 2, 1, 3).reshape(NB, NB)
    source = block_row // TRB * NCOLS + block_col // TCB
    target = (source + offsets[ranks % NDEV]) % NDEV
    return jnp.where(lower > 0, target, -1).astype(jnp.int32)


def place_ends(entries, own_key, least, largest):
    longest = entries.shape.index(max(entries.shape))
    spots = []
    for shift in (0, 1):
        where = [jax.random.randint(jax.random.fold_in(own_key, axis), (), 0, length) for axis, length in enumerate(entries.shape)]
        where[longest] = (where[longest] + shift) % entries.shape[longest]
        spots.append(tuple(where))
    return entries.at[spots[0]].set(least).at[spots[1]].set(largest)


def block_levels(own_key, extent, cuts, low, largest):
    level = 1.0
    for dim, shards_of in cuts:
        heights = jax.random.uniform(jax.random.fold_in(jax.random.fold_in(own_key, 6), dim), (shards_of,), jnp.float32, low / len(cuts), largest / len(cuts))
        level = level * jnp.repeat(jnp.exp(heights), extent[dim] // shards_of).reshape((-1,) + (1,) * (len(extent) - 1 - dim))
    return level


def bell_draw(rng, dims, width, bound, shards=(), kind=jnp.bfloat16):
    entries = width * jax.random.normal(rng, dims, jnp.float32)
    if shards:
        entries = entries * block_levels(rng, dims, shards, -0.22, 0.18)
    return jnp.clip(entries, -bound, bound).astype(kind)


def setup_inputs(seed: int = 0) -> dict:
    keys = jax.random.split(jax.random.key(seed), 6)
    return {
        "front": bell_draw(keys[0], (F, F), 1.0, 6.0, ((0, 8), (1, 16)), jnp.float32),
        "inverses": draw_inverses(jax.random.fold_in(keys[5], 71), 0),
        "block_owner": draw_block_owner(jax.random.fold_in(keys[5], 71), 0),
        "block_slot": place_ends(jax.random.randint(keys[3], (NB, NB), 0, PSLOT), jax.random.fold_in(keys[3], 1), 0, PSLOT - 1).astype(jnp.int32),
        "parent_in": bell_draw(keys[4], (PB, BS, BS), 1.0, 6.0, ((0, 128),), jnp.float32),
    }


def matmul(left_side, right_side):
    return jnp.dot(left_side, right_side, preferred_element_type=jnp.float32, precision=lax.Precision.HIGHEST)


def reference(front, inverses, block_owner, block_slot, parent_in):
    factor_one = matmul(front[:, 0:PW], inverses[0])
    partial_value = front - matmul(factor_one, front[0:PW, :])
    factor_two = matmul(partial_value[:, PW:2 * PW], inverses[1])
    updated = partial_value - matmul(factor_two, partial_value[PW:2 * PW, :])
    panels = jnp.concatenate([factor_one, factor_two], axis=1)
    blocks = updated.reshape(NB, BS, NB, BS).transpose(0, 2, 1, 3).reshape(NB * NB, BS, BS)
    owners = block_owner.reshape(NB * NB)
    targets = jnp.where(owners >= 0, owners * PSLOT + block_slot.reshape(NB * NB), PB).astype(jnp.int32)
    added = jnp.zeros(parent_in.shape, parent_in.dtype).at[targets].add(blocks, mode="drop")
    parent_out = parent_in + added
    return updated, panels, parent_out
```

```python
import functools

import jax
import jax.numpy as jnp
from jax import lax
from jax.experimental import pallas as pl
from jax.experimental.pallas import tpu as pltpu
from jax.sharding import PartitionSpec as P

AXES = ("row", "col")
MIB = 1024 * 1024


def device(xl, z, xh, y, core):
    return (xl * 4 + z) * 16 + xh * 8 + y * 2 + core


def pairs(move, keep=lambda *place: True):
    listed = []
    for xl in range(2):
        for z in range(4):
            for xh in range(2):
                for y in range(4):
                    for core in range(2):
                        place = (xl, z, xh, y, core)
                        if keep(*place):
                            listed.append((device(*place), device(*move(*place))))
    return listed


def send(value, move, keep=lambda *place: True):
    return lax.ppermute(value, AXES, pairs(move, keep))


def place():
    row = lax.axis_index("row")
    col = lax.axis_index("col")
    return row // 4, row % 4, col // 8, (col // 2) % 4, col % 2


def choose(index, options):
    value = options[-1]
    for number in range(len(options) - 2, -1, -1):
        value = jnp.where(index == number, options[number], value)
    return value


def assemble(index, own, before, after, across):
    size = own.shape[0]
    whole = jnp.zeros((4 * size,) + own.shape[1:], own.dtype)
    for shift, piece in ((0, own), (3, before), (1, after), (2, across)):
        whole = lax.dynamic_update_slice(whole, piece, (((index + shift) % 4) * size, 0))
    return whole


def spread_columns(columns):
    _, _, xh, y, core = place()
    size = columns.shape[0] // 4
    parts = [columns[k * size : (k + 1) * size] for k in range(4)]
    arrived = [
        send(
            parts[k],
            lambda xl, z, xh, y, core, k=k: (xl, z, xh, k, core),
            lambda xl, z, xh, y, core: xh == 0 and y == 0 and core == 0,
        )
        for k in (1, 2, 3)
    ]
    piece = choose(y, [parts[0]] + arrived)
    across = send(
        piece,
        lambda xl, z, xh, y, core: (xl, z, 1, y, core),
        lambda xl, z, xh, y, core: xh == 0 and core == 0,
    )
    piece = jnp.where(xh == 0, piece, across)
    around = [
        send(
            piece,
            lambda xl, z, xh, y, core, step=step: (xl, z, xh, (y + step) % 4, core),
            lambda xl, z, xh, y, core: core == 0,
        )
        for step in (1, 3, 2)
    ]
    whole = assemble(y, piece, around[0], around[1], around[2])
    other = send(
        whole, lambda xl, z, xh, y, core: (xl, z, xh, y, 1), lambda xl, z, xh, y, core: core == 0
    )
    return jnp.where(core == 0, whole, other)


def spread_rows(rows):
    xl, z, _, _, _ = place()
    size = rows.shape[0] // 4
    parts = [rows[k * size : (k + 1) * size] for k in range(4)]
    arrived = [
        send(
            parts[k],
            lambda xl, z, xh, y, core, k=k: (xl, k, xh, y, core),
            lambda xl, z, xh, y, core: xl == 0 and z == 0,
        )
        for k in (1, 2, 3)
    ]
    piece = choose(z, [parts[0]] + arrived)
    across = send(
        piece,
        lambda xl, z, xh, y, core: (1, z, xh, y, core),
        lambda xl, z, xh, y, core: xl == 0,
    )
    piece = jnp.where(xl == 0, piece, across)
    around = [
        send(piece, lambda xl, z, xh, y, core, step=step: (xl, (z + step) % 4, xh, y, core))
        for step in (1, 3, 2)
    ]
    return assemble(z, piece, around[0], around[1], around[2])


def product(left, right):
    return jnp.dot(left, right, preferred_element_type=jnp.float32, precision=lax.Precision.HIGH)


def halves(value):
    high = value.astype(jnp.bfloat16)
    low = (value - high.astype(jnp.float32)).astype(jnp.bfloat16)
    return high, low


def update_kernel(
    owner_ref, front_ref, left_one, left_two, right_one, right_two,
    updated_ref, outgoing_ref, high_one, low_one, high_two, low_two, result, whole_sem, block_sem,
):
    step = pl.program_id(0)
    steps = pl.num_programs(0)
    slot = lax.rem(step, 2)
    tile = result.shape[1]
    edge = outgoing_ref.shape[1]
    down, across = tile // edge, result.shape[2] // edge

    def whole_copy(at, number):
        return pltpu.make_async_copy(
            result.at[at], updated_ref.at[pl.ds(number * tile, tile)], whole_sem.at[at]
        )

    def block_copies(at, number, act):
        for i in range(down):
            for j in range(across):
                owner = owner_ref[number * down + i, j]

                @pl.when(owner >= 0)
                def _():
                    act(
                        pltpu.make_async_copy(
                            result.at[at, pl.ds(i * edge, edge), pl.ds(j * edge, edge)],
                            outgoing_ref.at[jnp.maximum(owner, 0)],
                            block_sem.at[at],
                        )
                    )

    def finish(at, number):
        whole_copy(at, number).wait()
        block_copies(at, number, lambda copy: copy.wait())

    @pl.when(step == 0)
    def _():
        high_one[...], low_one[...] = halves(right_one[...])
        high_two[...], low_two[...] = halves(right_two[...])

    @pl.when(step >= 2)
    def _():
        finish(slot, step - 2)

    total = front_ref[...]
    for left, high, low in ((left_one, high_one, low_one), (left_two, high_two, low_two)):
        left_high, left_low = halves(left[...])
        total -= (
            jnp.dot(left_high, low[...], preferred_element_type=jnp.float32)
            + jnp.dot(left_low, high[...], preferred_element_type=jnp.float32)
        ) + jnp.dot(left_high, high[...], preferred_element_type=jnp.float32)
    result[slot] = total
    whole_copy(slot, step).start()
    block_copies(slot, step, lambda copy: copy.start())

    @pl.when(step == steps - 1)
    def _():
        finish(1 - slot, step - 1)
        finish(slot, step)


def update(front, block_owner, left_one, left_two, right_one, right_two, devices, edge):
    rows, columns = front.shape
    depth = left_one.shape[1]
    tile = 2 * edge
    return pl.pallas_call(
        update_kernel,
        grid=(rows // tile,),
        in_specs=[
            pl.BlockSpec(memory_space=pltpu.SMEM),
            pl.BlockSpec((tile, columns), lambda i: (i, 0)),
            pl.BlockSpec((tile, depth), lambda i: (i, 0)),
            pl.BlockSpec((tile, depth), lambda i: (i, 0)),
            pl.BlockSpec((depth, columns), lambda i: (0, 0)),
            pl.BlockSpec((depth, columns), lambda i: (0, 0)),
        ],
        out_specs=[pl.BlockSpec(memory_space=pl.ANY), pl.BlockSpec(memory_space=pl.ANY)],
        out_shape=[
            jax.ShapeDtypeStruct((rows, columns), jnp.float32),
            jax.ShapeDtypeStruct((devices, edge, edge), jnp.float32),
        ],
        scratch_shapes=[pltpu.VMEM((depth, columns), jnp.bfloat16)] * 4
        + [
            pltpu.VMEM((2, tile, columns), jnp.float32),
            pltpu.SemaphoreType.DMA((2,)),
            pltpu.SemaphoreType.DMA((2,)),
        ],
        compiler_params=pltpu.CompilerParams(vmem_limit_bytes=40 * MIB),
        cost_estimate=pl.CostEstimate(
            flops=12 * rows * columns * depth, bytes_accessed=32 * MIB, transcendentals=0
        ),
        name="update",
    )(block_owner, front, left_one, left_two, right_one, right_two)


def add_kernel(slot_ref, parent_ref, arrived_ref, out_ref):
    step = pl.program_id(0)
    count = arrived_ref.shape[0]

    @pl.when(step == 0)
    def _():
        out_ref[...] = parent_ref[...]

    for k in range(count):
        slot = slot_ref[step * count + k]

        @pl.when(slot >= 0)
        def _():
            at = jnp.maximum(slot, 0)
            out_ref[at] = out_ref[at] + arrived_ref[k]


def extend_add(slots, parent, arrived):
    count = 8
    held, edge, _ = parent.shape
    return pl.pallas_call(
        add_kernel,
        grid=(arrived.shape[0] // count,),
        in_specs=[
            pl.BlockSpec(memory_space=pltpu.SMEM),
            pl.BlockSpec((held, edge, edge), lambda i: (0, 0, 0)),
            pl.BlockSpec((count, edge, edge), lambda i: (i, 0, 0)),
        ],
        out_specs=pl.BlockSpec((held, edge, edge), lambda i: (0, 0, 0)),
        out_shape=jax.ShapeDtypeStruct(parent.shape, jnp.float32),
        compiler_params=pltpu.CompilerParams(vmem_limit_bytes=32 * MIB),
        cost_estimate=pl.CostEstimate(flops=2 * MIB, bytes_accessed=14 * MIB, transcendentals=0),
        name="extend_add",
    )(slots, parent, arrived)


def local(front, inverses, block_owner, block_slot, parent_in):
    width = inverses.shape[1]
    edge = parent_in.shape[1]
    devices = lax.axis_size("row") * lax.axis_size("col")

    owners = block_owner.reshape(-1)
    slots = block_slot.reshape(-1)
    named = owners[None, :] == jnp.arange(devices, dtype=jnp.int32)[:, None]
    labels = jnp.sum(jnp.where(named, slots[None, :] + 1, 0), axis=1) - 1
    markers = lax.all_to_all(labels.reshape(devices, 1, 1), AXES, 0, 0, tiled=True).reshape(devices)

    columns_one = front[:, :width]
    rows_one = product(inverses[0], front[:width])
    left_one = spread_columns(columns_one)
    right_one = spread_rows(rows_one)

    columns_two = front[:, width : 2 * width] - product(columns_one, right_one[:, width : 2 * width])
    rows_two = front[width : 2 * width] - product(left_one[width : 2 * width], right_one)
    rows_two = product(inverses[1], rows_two)
    left_two = spread_columns(columns_two)
    right_two = spread_rows(rows_two)

    updated, outgoing = update(
        front, block_owner, left_one, left_two, right_one, right_two, devices, edge
    )
    arrived = lax.all_to_all(outgoing, AXES, 0, 0, tiled=True)

    piece = front.shape[0] // lax.axis_size("col")
    start = lax.axis_index("col") * piece
    panels = jnp.concatenate(
        [
            product(lax.dynamic_slice_in_dim(left_one, start, piece, 0), inverses[0]),
            product(lax.dynamic_slice_in_dim(left_two, start, piece, 0), inverses[1]),
        ],
        axis=1,
    )
    parent_out = extend_add(markers, parent_in, arrived)
    return (updated, panels, parent_out)


def solution(mesh):
    in_specs = (
        P("row", "col"),
        P(),
        P("row", "col"),
        P("row", "col"),
        P(("row", "col"), None, None),
    )
    out_specs = (P("row", "col"), P(("row", "col"), None), P(("row", "col"), None, None))
    return jax.shard_map(local, mesh=mesh, in_specs=in_specs, out_specs=out_specs, check_vma=False)
```

```python
import jax
import jax.numpy as jnp
from jax import lax
from jax.experimental import pallas as pl
from jax.experimental.pallas import tpu as pltpu
from jax.sharding import PartitionSpec as P

AXES = ("row", "col")
MIB = 1024 * 1024


def device(xl, z, xh, y, core):
    return (xl * 4 + z) * 16 + xh * 8 + y * 2 + core


def pairs(move, keep=lambda *place: True):
    listed = []
    for xl in range(2):
        for z in range(4):
            for xh in range(2):
                for y in range(4):
                    for core in range(2):
                        place = (xl, z, xh, y, core)
                        if keep(*place):
                            listed.append((device(*place), device(*move(*place))))
    return listed


def send(value, move, keep=lambda *place: True):
    return lax.ppermute(value, AXES, pairs(move, keep))


def place():
    row = lax.axis_index("row")
    col = lax.axis_index("col")
    return row // 4, row % 4, col // 8, (col // 2) % 4, col % 2


def choose(index, options):
    value = options[-1]
    for number in range(len(options) - 2, -1, -1):
        value = jnp.where(index == number, options[number], value)
    return value


def partner(k, first):
    return k ^ 1 if first else 3 - k


def exchange(columns, rows):
    xl, z, xh, y, core = place()
    edge = columns.shape[0] // 8
    parts = [columns[k * edge : (k + 1) * edge] for k in range(8)]
    lift = rows.shape[0] // 4
    layers = [rows[k * lift : (k + 1) * lift] for k in range(4)]

    came_columns = {}
    came_rows = {}
    for k in (2, 1, 3):
        for to in range(2):
            came_columns[2 * k + to] = send(
                parts[2 * k + to],
                lambda xl, z, xh, y, core, k=k, to=to: (xl, z, xh, k, to),
                lambda xl, z, xh, y, core: xh == 0 and y == 0 and core == 0,
            )
    for k in (2, 1, 3):
        came_rows[k] = send(
            layers[k],
            lambda xl, z, xh, y, core, k=k: (xl, k, xh, y, core),
            lambda xl, z, xh, y, core: xl == 0 and z == 0,
        )
    came_columns[1] = send(
        parts[1],
        lambda xl, z, xh, y, core: (xl, z, xh, y, 1),
        lambda xl, z, xh, y, core: xh == 0 and y == 0 and core == 0,
    )
    column = choose(2 * y + core, [parts[0]] + [came_columns[k] for k in range(1, 8)])
    row = choose(z, [layers[0]] + [came_rows[k] for k in range(1, 4)])
    column, row = lax.optimization_barrier((column, row))

    column_across = send(
        column,
        lambda xl, z, xh, y, core: (xl, z, 1, y, core),
        lambda xl, z, xh, y, core: xh == 0,
    )
    row_across = send(
        row,
        lambda xl, z, xh, y, core: (1, z, xh, y, core),
        lambda xl, z, xh, y, core: xl == 0,
    )
    column = jnp.where(xh == 0, column, column_across)
    row = jnp.where(xl == 0, row, row_across)
    column, row = lax.optimization_barrier((column, row))

    def around(value, step):
        return send(
            value,
            lambda xl, z, xh, y, core: (xl, z, xh, partner(y, (core == 0) == (step == 0)), core),
        )

    def along(value, step):
        return send(
            value,
            lambda xl, z, xh, y, core: (xl, partner(z, (core == 0) == (step == 0)), xh, y, core),
        )

    def swap(value):
        return send(value, lambda xl, z, xh, y, core: (xl, z, xh, y, 1 - core))

    column_a, row_a = around(column, 0), along(row, 0)
    column_b, row_b = around(column, 1), along(row, 1)
    other = swap(column)
    column_a, row_a = lax.optimization_barrier((column_a, row_a))
    column_c, row_c = around(column_a, 1), along(row_a, 1)
    other_a, other_b = swap(column_a), swap(column_b)
    other_c = swap(column_c)

    def order(k, core):
        one = jnp.where(core == 0, k ^ 1, 3 - k)
        two = jnp.where(core == 0, 3 - k, k ^ 1)
        return [k, one, two, 3 - (k ^ 1)]

    pieces = [column, other, column_a, column_b, other_a, other_b, column_c, other_c]
    mine, theirs = order(y, core), order(y, 1 - core)
    numbers = [
        2 * mine[0] + core,
        2 * theirs[0] + 1 - core,
        2 * mine[1] + core,
        2 * mine[2] + core,
        2 * theirs[1] + 1 - core,
        2 * theirs[2] + 1 - core,
        2 * mine[3] + core,
        2 * theirs[3] + 1 - core,
    ]
    return pieces, numbers, [row, row_a, row_b, row_c], order(z, core)


def halves(value):
    high = value.astype(jnp.bfloat16)
    low = (value - high.astype(jnp.float32)).astype(jnp.bfloat16)
    return high, low


def dot(left, right):
    return jnp.dot(left, right, preferred_element_type=jnp.float32)


def product(left, right):
    left_high, left_low = halves(left)
    right_high, right_low = halves(right)
    return dot(left_high, right_low) + dot(left_low, right_high) + dot(left_high, right_high)


def update_kernel(
    table_ref, owner_ref, front_ref, pivot_ref, inverse_ref, *refs
):
    column_refs = refs[:8]
    row_refs = refs[8:12]
    updated_ref, outgoing_ref, mine_ref = refs[12:15]
    right, high, low, held, result, held_sem, whole_sem, block_sem = refs[15:]
    step = pl.program_id(0)
    steps = pl.num_programs(0)
    slot = lax.rem(step, 2)
    tile = result.shape[1]
    edge = outgoing_ref.shape[1]
    depth = inverse_ref.shape[0]
    down, across = tile // edge, result.shape[2] // edge

    def fetch(number, at):
        return pltpu.make_async_copy(column_refs[number], held.at[at], held_sem.at[at])

    def whole_copy(at, number):
        top = pl.multiple_of(table_ref[number] * tile, tile)
        return pltpu.make_async_copy(
            result.at[at], updated_ref.at[pl.ds(top, tile)], whole_sem.at[at]
        )

    def block_copies(at, number, act):
        for i in range(down):
            for j in range(across):
                owner = owner_ref[table_ref[number] * down + i, j]

                @pl.when(owner >= 0)
                def _():
                    act(
                        pltpu.make_async_copy(
                            result.at[at, pl.ds(i * edge, edge), pl.ds(j * edge, edge)],
                            outgoing_ref.at[jnp.maximum(owner, 0)],
                            block_sem.at[at],
                        )
                    )

    def finish(at, number):
        whole_copy(at, number).wait()
        block_copies(at, number, lambda copy: copy.wait())

    @pl.when(step == 0)
    def _():
        fetch(0, 0).start()
        lift = row_refs[0].shape[0]
        for k in range(4):
            top = pl.multiple_of(table_ref[8 + k] * lift, lift)
            right[pl.ds(top, lift)] = row_refs[k][...]
        one = right[:depth]
        two = right[depth:] - product(pivot_ref[depth:], one)
        two = product(inverse_ref[...], two)
        high[depth:], low[depth:] = halves(two)
        one = one - product(pivot_ref[:depth], two)
        high[:depth], low[:depth] = halves(one)

    for number in range(8):

        @pl.when(step == number)
        def _():
            if number < 7:
                fetch(number + 1, (number + 1) % 2).start()
            fetch(number, number % 2).wait()

    @pl.when(step >= 2)
    def _():
        finish(slot, step - 2)

    left = held[slot]
    left_high, left_low = halves(left)
    total = front_ref[...] - dot(left_high, low[...])
    total -= dot(left_low, high[...])
    total -= dot(left_high, high[...])
    result[slot] = total
    whole_copy(slot, step).start()
    block_copies(slot, step, lambda copy: copy.start())

    @pl.when(table_ref[step] == table_ref[12])
    def _():
        top = pl.multiple_of(table_ref[13] * edge, edge)
        mine_ref[...] = held[slot, pl.ds(top, edge)]

    @pl.when(step == steps - 1)
    def _():
        finish(1 - slot, step - 1)
        finish(slot, step)


def update(front, block_owner, pivot, inverse, pieces, layers, table, devices, edge):
    rows, columns = front.shape
    tile = pieces[0].shape[0]
    whole = lambda *shape: pl.BlockSpec(shape, lambda i, table: (0,) * len(shape))
    return pl.pallas_call(
        update_kernel,
        grid_spec=pltpu.PrefetchScalarGridSpec(
            num_scalar_prefetch=1,
            grid=(rows // tile,),
            in_specs=[
                pl.BlockSpec(memory_space=pltpu.SMEM),
                pl.BlockSpec((tile, columns), lambda i, table: (table[i], 0)),
                whole(*pivot.shape),
                whole(*inverse.shape),
            ]
            + [pl.BlockSpec(memory_space=pl.ANY)] * 8
            + [whole(*layers[0].shape)] * 4,
            out_specs=[
                pl.BlockSpec(memory_space=pl.ANY),
                pl.BlockSpec(memory_space=pl.ANY),
                whole(edge, pieces[0].shape[1]),
            ],
            scratch_shapes=[
                pltpu.VMEM((2 * inverse.shape[0], columns), jnp.float32),
                pltpu.VMEM((2 * inverse.shape[0], columns), jnp.bfloat16),
                pltpu.VMEM((2 * inverse.shape[0], columns), jnp.bfloat16),
                pltpu.VMEM((2, tile, pieces[0].shape[1]), jnp.float32),
                pltpu.VMEM((2, tile, columns), jnp.float32),
                pltpu.SemaphoreType.DMA((2,)),
                pltpu.SemaphoreType.DMA((2,)),
                pltpu.SemaphoreType.DMA((2,)),
            ],
        ),
        out_shape=[
            jax.ShapeDtypeStruct((rows, columns), jnp.float32),
            jax.ShapeDtypeStruct((devices, edge, edge), jnp.float32),
            jax.ShapeDtypeStruct((edge, pieces[0].shape[1]), jnp.float32),
        ],
        compiler_params=pltpu.CompilerParams(vmem_limit_bytes=44 * MIB),
        cost_estimate=pl.CostEstimate(
            flops=16 * rows * columns * inverse.shape[0],
            bytes_accessed=40 * MIB,
            transcendentals=0,
        ),
        name="update",
    )(table, block_owner, front, pivot, inverse, *pieces, *layers)


def add_kernel(slot_ref, parent_ref, arrived_ref, out_ref, sem):
    step = pl.program_id(0)
    count = arrived_ref.shape[0]

    @pl.when(step == 0)
    def _():
        copy = pltpu.make_async_copy(parent_ref, out_ref, sem)
        copy.start()
        copy.wait()

    for k in range(count):
        slot = slot_ref[step * count + k]

        @pl.when(slot >= 0)
        def _():
            at = jnp.maximum(slot, 0)
            out_ref[at] = out_ref[at] + arrived_ref[k]


def extend_add(slots, parent, arrived):
    count = 16
    held, edge, _ = parent.shape
    return pl.pallas_call(
        add_kernel,
        grid=(arrived.shape[0] // count,),
        in_specs=[
            pl.BlockSpec(memory_space=pltpu.SMEM),
            pl.BlockSpec(memory_space=pl.ANY),
            pl.BlockSpec((count, edge, edge), lambda i: (i, 0, 0)),
        ],
        out_specs=pl.BlockSpec((held, edge, edge), lambda i: (0, 0, 0)),
        out_shape=jax.ShapeDtypeStruct(parent.shape, jnp.float32),
        scratch_shapes=[pltpu.SemaphoreType.DMA],
        compiler_params=pltpu.CompilerParams(vmem_limit_bytes=32 * MIB),
        cost_estimate=pl.CostEstimate(flops=2 * MIB, bytes_accessed=14 * MIB, transcendentals=0),
        name="extend_add",
    )(slots, parent, arrived)


def exact(left, right):
    return jnp.dot(left, right, preferred_element_type=jnp.float32, precision=lax.Precision.HIGHEST)


def local(front, inverses, block_owner, block_slot, parent_in):
    width = inverses.shape[1]
    edge = parent_in.shape[1]
    devices = lax.axis_size("row") * lax.axis_size("col")
    row, col = lax.axis_index("row"), lax.axis_index("col")
    me = row * lax.axis_size("col") + col

    columns = front[:, : 2 * width]
    rows_one = product_rows(inverses[0], front[:width])
    rows = jnp.concatenate([rows_one, front[width : 2 * width]], axis=0)

    owners = block_owner.reshape(-1)
    slots = block_slot.reshape(-1)
    names = jnp.arange(devices, dtype=jnp.int32)
    named = owners[None, :] == names[:, None]
    labels = jnp.sum(jnp.where(named, slots[None, :] + 1, 0), axis=1).astype(jnp.float32)
    labels = jnp.where(names[None, :] == me, labels[:, None], 0.0)
    pivot = jnp.concatenate(
        [rows_one[:, width : 2 * width], front[width : 2 * width, :width]], axis=0
    )
    pivot = jnp.where(me == 0, pivot, 0.0)
    fill = devices * devices // width
    shared = lax.psum(jnp.concatenate([pivot, labels.reshape(fill, width)], axis=0), AXES)
    pivot = shared[: 2 * width]
    markers = shared[2 * width :].reshape(devices, devices)
    markers = lax.dynamic_slice_in_dim(markers, me, 1, 0).reshape(devices).astype(jnp.int32) - 1

    pieces, numbers, layers, heights = exchange(columns, rows)
    table = jnp.stack(numbers + heights + [col // 2, col % 2]).astype(jnp.int32)
    updated, outgoing, mine = update(
        front, block_owner, pivot, inverses[1], pieces, layers, table, devices, edge
    )
    arrived = lax.all_to_all(outgoing, AXES, 0, 0, tiled=True)

    mine_one, mine_two = mine[:, :width], mine[:, width:]
    mine_two = mine_two - exact(mine_one, pivot[:width])
    panels = jnp.concatenate([exact(mine_one, inverses[0]), exact(mine_two, inverses[1])], axis=1)
    parent_out = extend_add(markers, parent_in, arrived)
    return (updated, panels, parent_out)


def product_rows(left, right):
    return jnp.dot(left, right, preferred_element_type=jnp.float32, precision=lax.Precision.HIGH)


def solution(mesh):
    in_specs = (
        P("row", "col"),
        P(),
        P("row", "col"),
        P("row", "col"),
        P(("row", "col"), None, None),
    )
    out_specs = (P("row", "col"), P(("row", "col"), None), P(("row", "col"), None, None))
    return jax.shard_map(local, mesh=mesh, in_specs=in_specs, out_specs=out_specs, check_vma=False)
```

```python
import jax
import jax.numpy as jnp
from jax import lax
from jax.experimental import pallas as pl
from jax.experimental.pallas import tpu as pltpu
from jax.sharding import PartitionSpec as P

AXES = ("row", "col")
MIB = 1024 * 1024


def device(xl, z, xh, y, core):
    return (xl * 4 + z) * 16 + xh * 8 + y * 2 + core


def pairs(move, keep=lambda *place: True):
    listed = []
    for xl in range(2):
        for z in range(4):
            for xh in range(2):
                for y in range(4):
                    for core in range(2):
                        place = (xl, z, xh, y, core)
                        if keep(*place):
                            listed.append((device(*place), device(*move(*place))))
    return listed


def send(value, move, keep=lambda *place: True):
    return lax.ppermute(value, AXES, pairs(move, keep))


def place():
    row = lax.axis_index("row")
    col = lax.axis_index("col")
    return row // 4, row % 4, col // 8, (col // 2) % 4, col % 2


def choose(index, options):
    value = options[-1]
    for number in range(len(options) - 2, -1, -1):
        value = jnp.where(index == number, options[number], value)
    return value


def partner(k, first):
    return k ^ 1 if first else 3 - k


def exchange(columns, rows, deal, spread_pivot):
    xl, z, xh, y, core = place()
    edge = columns.shape[0] // 8
    lift = rows.shape[0] // 4
    parts = [columns[2 * k * edge : 2 * (k + 1) * edge] for k in range(4)]
    layers = [rows[k * lift : (k + 1) * lift] for k in range(4)]

    came_columns = [
        send(
            parts[k],
            lambda xl, z, xh, y, core, k=k: (xl, z, xh, k, core),
            lambda xl, z, xh, y, core: xh == 0 and y == 0 and core == 0,
        )
        for k in (1, 2, 3)
    ]
    came_rows = [
        send(
            layers[k],
            lambda xl, z, xh, y, core, k=k: (xl, k, xh, y, core),
            lambda xl, z, xh, y, core: xl == 0 and z == 0,
        )
        for k in (1, 2, 3)
    ]
    dealt = lax.all_to_all(deal, AXES, 0, 0, tiled=True)
    part = [
        choose(y, [one[k * edge : (k + 1) * edge] for one in [parts[0]] + came_columns])
        for k in range(2)
    ]
    row = choose(z, [layers[0]] + came_rows)
    part, row, dealt = lax.optimization_barrier((part, row, dealt))

    row_across = send(
        row,
        lambda xl, z, xh, y, core: (1, z, xh, y, core),
        lambda xl, z, xh, y, core: xl == 0,
    )
    from_core = lambda xl, z, xh, y, core: xh == 0 and core == 0
    across = [
        send(part[k], lambda xl, z, xh, y, core, k=k: (xl, z, 1, y, k), from_core) for k in range(2)
    ]
    beside = send(part[1], lambda xl, z, xh, y, core: (xl, z, xh, y, 1), from_core)
    column = jnp.where(
        xh == 0, jnp.where(core == 0, part[0], beside), jnp.where(core == 0, across[0], across[1])
    )
    row = jnp.where(xl == 0, row, row_across)
    column, row = lax.optimization_barrier((column, row))
    pivot = spread_pivot(dealt)

    def around(value, step):
        return send(
            value,
            lambda xl, z, xh, y, core: (xl, z, xh, partner(y, (core == 0) == (step == 0)), core),
        )

    def along(value, step):
        return send(
            value,
            lambda xl, z, xh, y, core: (xl, partner(z, (core == 0) == (step == 0)), xh, y, core),
        )

    def swap(value):
        return send(value, lambda xl, z, xh, y, core: (xl, z, xh, y, 1 - core))

    row_a, column_a = along(row, 0), around(column, 0)
    row_b, column_b = along(row, 1), around(column, 1)
    other = swap(column)
    column_a, row_a, pivot = lax.optimization_barrier((column_a, row_a, pivot))
    row_c, column_c = along(row_a, 1), around(column_a, 1)
    other_a, other_b = swap(column_a), swap(column_b)
    other_c = swap(column_c)

    def order(k, core):
        one = jnp.where(core == 0, k ^ 1, 3 - k)
        two = jnp.where(core == 0, 3 - k, k ^ 1)
        return [k, one, two, 3 - (k ^ 1)]

    pieces = [column, other, column_a, column_b, other_a, other_b, column_c, other_c]
    mine, theirs = order(y, core), order(y, 1 - core)
    numbers = [
        2 * mine[0] + core,
        2 * theirs[0] + 1 - core,
        2 * mine[1] + core,
        2 * mine[2] + core,
        2 * theirs[1] + 1 - core,
        2 * theirs[2] + 1 - core,
        2 * mine[3] + core,
        2 * theirs[3] + 1 - core,
    ]
    return pieces, numbers, [row, row_a, row_b, row_c], order(z, core), dealt, pivot


def halves(value):
    high = value.astype(jnp.bfloat16)
    low = (value - high.astype(jnp.float32)).astype(jnp.bfloat16)
    return high, low


def dot(left, right):
    return jnp.dot(left, right, preferred_element_type=jnp.float32)


def product(left, right):
    left_high, left_low = halves(left)
    right_high, right_low = halves(right)
    return dot(left_high, right_low) + dot(left_low, right_high) + dot(left_high, right_high)


def update_kernel(
    table_ref, owner_ref, front_ref, pivot_ref, inverse_ref, *refs
):
    column_refs = refs[:8]
    row_refs = refs[8:12]
    updated_ref, outgoing_ref, mine_ref = refs[12:15]
    right, high, low, held, result, held_sem, whole_sem, block_sem = refs[15:]
    step = pl.program_id(0)
    steps = pl.num_programs(0)
    slot = lax.rem(step, 2)
    tile = result.shape[1]
    edge = outgoing_ref.shape[1]
    depth = inverse_ref.shape[1]
    down, across = tile // edge, result.shape[2] // edge

    def fetch(number, at):
        return pltpu.make_async_copy(column_refs[number], held.at[at], held_sem.at[at])

    def whole_copy(at, number):
        top = pl.multiple_of(table_ref[number] * tile, tile)
        return pltpu.make_async_copy(
            result.at[at], updated_ref.at[pl.ds(top, tile)], whole_sem.at[at]
        )

    def block_copies(at, number, act):
        for i in range(down):
            for j in range(across):
                owner = owner_ref[table_ref[number] * down + i, j]

                @pl.when(owner >= 0)
                def _():
                    act(
                        pltpu.make_async_copy(
                            result.at[at, pl.ds(i * edge, edge), pl.ds(j * edge, edge)],
                            outgoing_ref.at[jnp.maximum(owner, 0)],
                            block_sem.at[at],
                        )
                    )

    def finish(at, number):
        whole_copy(at, number).wait()
        block_copies(at, number, lambda copy: copy.wait())

    @pl.when(step == 0)
    def _():
        fetch(0, 0).start()
        lift = row_refs[0].shape[0]
        for k in range(4):
            top = pl.multiple_of(table_ref[8 + k] * lift, lift)
            right[pl.ds(top, lift)] = row_refs[k][...]
        side = pivot_ref.shape[1]
        pivot = [
            jnp.concatenate(
                [
                    pivot_ref[k * 2 * depth + half * depth : k * 2 * depth + (half + 1) * depth]
                    for k in range(depth // side)
                ],
                axis=1,
            )
            for half in range(2)
        ]
        one = right[:depth]
        two = right[depth:] - product(pivot[1], one)
        two = product(inverse_ref[0], two)
        high[depth:], low[depth:] = halves(two)
        one = one - product(pivot[0], two)
        high[:depth], low[:depth] = halves(one)

    for number in range(8):

        @pl.when(step == number)
        def _():
            if number < 7:
                fetch(number + 1, (number + 1) % 2).start()
            fetch(number, number % 2).wait()

    @pl.when(step >= 2)
    def _():
        finish(slot, step - 2)

    left = held[slot]
    left_high, left_low = halves(left)
    total = front_ref[...] - dot(left_high, low[...])
    total -= dot(left_low, high[...])
    total -= dot(left_high, high[...])
    result[slot] = total
    whole_copy(slot, step).start()
    block_copies(slot, step, lambda copy: copy.start())

    @pl.when(table_ref[step] == table_ref[12])
    def _():
        top = pl.multiple_of(table_ref[13] * edge, edge)
        mine_ref[...] = held[slot, pl.ds(top, edge)]

    @pl.when(step == steps - 1)
    def _():
        finish(1 - slot, step - 1)
        finish(slot, step)


def update(front, block_owner, pivot, inverses, pieces, layers, table, devices, edge):
    rows, columns = front.shape
    depth = inverses.shape[1]
    tile = pieces[0].shape[0]
    whole = lambda *shape: pl.BlockSpec(shape, lambda i, table: (0,) * len(shape))
    return pl.pallas_call(
        update_kernel,
        grid_spec=pltpu.PrefetchScalarGridSpec(
            num_scalar_prefetch=1,
            grid=(rows // tile,),
            in_specs=[
                pl.BlockSpec(memory_space=pltpu.SMEM),
                pl.BlockSpec((tile, columns), lambda i, table: (table[i], 0)),
                whole(*pivot.shape),
                pl.BlockSpec((1,) + inverses.shape[1:], lambda i, table: (1, 0, 0)),
            ]
            + [pl.BlockSpec(memory_space=pl.ANY)] * 8
            + [whole(*layers[0].shape)] * 4,
            out_specs=[
                pl.BlockSpec(memory_space=pl.ANY),
                pl.BlockSpec(memory_space=pl.ANY),
                whole(edge, pieces[0].shape[1]),
            ],
            scratch_shapes=[
                pltpu.VMEM((2 * depth, columns), jnp.float32),
                pltpu.VMEM((2 * depth, columns), jnp.bfloat16),
                pltpu.VMEM((2 * depth, columns), jnp.bfloat16),
                pltpu.VMEM((2, tile, pieces[0].shape[1]), jnp.float32),
                pltpu.VMEM((2, tile, columns), jnp.float32),
                pltpu.SemaphoreType.DMA((2,)),
                pltpu.SemaphoreType.DMA((2,)),
                pltpu.SemaphoreType.DMA((2,)),
            ],
        ),
        out_shape=[
            jax.ShapeDtypeStruct((rows, columns), jnp.float32),
            jax.ShapeDtypeStruct((devices, edge, edge), jnp.float32),
            jax.ShapeDtypeStruct((edge, pieces[0].shape[1]), jnp.float32),
        ],
        compiler_params=pltpu.CompilerParams(vmem_limit_bytes=44 * MIB),
        cost_estimate=pl.CostEstimate(
            flops=16 * rows * columns * depth,
            bytes_accessed=40 * MIB,
            transcendentals=0,
        ),
        name="update",
    )(table, block_owner, front, pivot, inverses, *pieces, *layers)


def add_kernel(slot_ref, parent_ref, arrived_ref, out_ref, sem):
    step = pl.program_id(0)
    count = arrived_ref.shape[0]

    @pl.when(step == 0)
    def _():
        copy = pltpu.make_async_copy(parent_ref, out_ref, sem)
        copy.start()
        copy.wait()

    for k in range(count):
        slot = slot_ref[step * count + k]

        @pl.when(slot >= 0)
        def _():
            at = jnp.maximum(slot, 0)
            out_ref[at] = out_ref[at] + arrived_ref[k]


def extend_add(slots, parent, arrived):
    count = 16
    held, edge, _ = parent.shape
    return pl.pallas_call(
        add_kernel,
        grid=(arrived.shape[0] // count,),
        in_specs=[
            pl.BlockSpec(memory_space=pltpu.SMEM),
            pl.BlockSpec(memory_space=pl.ANY),
            pl.BlockSpec((count, edge, edge), lambda i: (i, 0, 0)),
        ],
        out_specs=pl.BlockSpec((held, edge, edge), lambda i: (0, 0, 0)),
        out_shape=jax.ShapeDtypeStruct(parent.shape, jnp.float32),
        scratch_shapes=[pltpu.SemaphoreType.DMA],
        compiler_params=pltpu.CompilerParams(vmem_limit_bytes=32 * MIB),
        cost_estimate=pl.CostEstimate(flops=2 * MIB, bytes_accessed=14 * MIB, transcendentals=0),
        name="extend_add",
    )(slots, parent, arrived)


def exact(left, right):
    return jnp.dot(left, right, preferred_element_type=jnp.float32, precision=lax.Precision.HIGHEST)


def local(front, inverses, block_owner, block_slot, parent_in):
    width = inverses.shape[1]
    edge = parent_in.shape[1]
    devices = lax.axis_size("row") * lax.axis_size("col")
    col = lax.axis_index("col")

    columns = front[:, : 2 * width]
    rows_one = product_rows(inverses[0], front[:width])
    rows = jnp.concatenate([rows_one, front[width : 2 * width]], axis=0)

    owners = block_owner.reshape(-1)
    slots = block_slot.reshape(-1)
    named = owners[None, :] == jnp.arange(devices, dtype=jnp.int32)[:, None]
    labels = jnp.sum(jnp.where(named, slots[None, :] + 1, 0), axis=1).astype(jnp.float32)
    labels = jnp.broadcast_to(labels[:, None, None], (devices, 8, edge))
    pivot = jnp.concatenate(
        [rows_one[:, width : 2 * width], front[width : 2 * width, :width]], axis=0
    )
    pivot = pivot.reshape(2 * width, width // edge, edge).transpose(1, 0, 2)
    pivot = pivot.reshape(devices, -1, edge)
    deal = jnp.concatenate([pivot, labels], axis=1)
    share = pivot.shape[1]

    def spread_pivot(dealt):
        copies = jnp.broadcast_to(dealt[:1, :share], pivot.shape)
        return lax.all_to_all(copies, AXES, 0, 0, tiled=True).reshape(-1, edge)

    pieces, numbers, layers, heights, dealt, pivot = exchange(columns, rows, deal, spread_pivot)
    markers = dealt[:, share, 0].astype(jnp.int32) - 1
    table = jnp.stack(numbers + heights + [col // 2, col % 2]).astype(jnp.int32)
    updated, outgoing, mine = update(
        front, block_owner, pivot, inverses, pieces, layers, table, devices, edge
    )
    arrived = lax.all_to_all(outgoing, AXES, 0, 0, tiled=True)

    mine_one, mine_two = mine[:, :width], mine[:, width:]
    corner = pivot.reshape(width // edge, 2 * width, edge)[:, :width]
    corner = corner.transpose(1, 0, 2).reshape(width, width)
    mine_two = mine_two - exact(mine_one, corner)
    panels = jnp.concatenate([exact(mine_one, inverses[0]), exact(mine_two, inverses[1])], axis=1)
    parent_out = extend_add(markers, parent_in, arrived)
    return (updated, panels, parent_out)


def product_rows(left, right):
    return jnp.dot(left, right, preferred_element_type=jnp.float32, precision=lax.Precision.HIGH)


def solution(mesh):
    in_specs = (
        P("row", "col"),
        P(),
        P("row", "col"),
        P("row", "col"),
        P(("row", "col"), None, None),
    )
    out_specs = (P("row", "col"), P(("row", "col"), None), P(("row", "col"), None, None))
    return jax.shard_map(local, mesh=mesh, in_specs=in_specs, out_specs=out_specs, check_vma=False)
```

```python
import jax
import jax.numpy as jnp
from jax import lax
from jax.experimental import pallas as pl
from jax.experimental.pallas import tpu as pltpu
from jax.sharding import PartitionSpec as P

AXES = ("row", "col")
MIB = 1024 * 1024


def device(xl, z, xh, y, core):
    return (xl * 4 + z) * 16 + xh * 8 + y * 2 + core


def pairs(move, keep=lambda *place: True):
    listed = []
    for xl in range(2):
        for z in range(4):
            for xh in range(2):
                for y in range(4):
                    for core in range(2):
                        place = (xl, z, xh, y, core)
                        if keep(*place):
                            listed.append((device(*place), device(*move(*place))))
    return listed


def send(value, move, keep=lambda *place: True):
    return lax.ppermute(value, AXES, pairs(move, keep))


def place():
    row = lax.axis_index("row")
    col = lax.axis_index("col")
    return row // 4, row % 4, col // 8, (col // 2) % 4, col % 2


def partner(k, first):
    return k ^ 1 if first else 3 - k


STEPS = ("z0", "z1", "y0", "y1", "xl", "xh")


def moved(spot, step):
    xl, z, xh, y = spot
    if step[0] == "z":
        return (xl, partner(z, step == "z0"), xh, y)
    if step[0] == "y":
        return (xl, z, xh, partner(y, step == "y0"))
    return (1 - xl, z, xh, y) if step == "xl" else (xl, z, 1 - xh, y)


def doubling():
    orders = (STEPS, STEPS[2:4] + STEPS[:2] + ("xh", "xl"))
    having = [{(0, 0, 0, 0)}, {(0, 0, 0, 0)}]
    rounds = []
    for number in range(6):
        listed = []
        for core in range(2):
            new = {moved(spot, orders[core][number]): spot for spot in sorted(having[core])}
            for to, start in new.items():
                listed.append((device(*start, core), device(*to, core)))
            having[core] = having[core] | set(new)
        rounds.append(listed)
    return rounds


def exchange(columns, rows, pivot_one, pivot_two, labels):
    xl, z, xh, y, core = place()
    first = core == 0
    edge = columns.shape[0] // 8
    lift = rows.shape[0] // 4
    part = lambda k, count=1: columns[k * edge : (k + count) * edge]
    layer = lambda k, count=1: rows[k * lift : (k + count) * lift]
    rounds = doubling()
    corner = ((xl == 0) & (z == 0)) & ((xh == 0) & (y == 0))

    def swap(value):
        return send(value, lambda xl, z, xh, y, core: (xl, z, xh, y, 1 - core))

    def spread(value, number):
        return value + lax.ppermute(value, AXES, rounds[number])

    source = lambda xl, z, xh, y, core: xh == 0 and y == 0 and core == 0

    one = send(part(1, 2), lambda xl, z, xh, y, core: (xl, z, xh, 1, 0), source)
    two = send(part(6, 2), lambda xl, z, xh, y, core: (xl, z, xh, 3, 1), source)
    low = send(
        jnp.where(first, layer(1, 2), layer(2, 2)),
        lambda xl, z, xh, y, core: (xl, partner(z, core == 0), xh, y, core),
        lambda xl, z, xh, y, core: xl == 0 and z == 0,
    )
    beside = lax.ppermute(pivot_two, AXES, [(0, 1)])
    pivot = jnp.where(corner & first, pivot_one, beside)
    pivot = spread(pivot, 0)
    one, two, low, pivot = lax.optimization_barrier((one, two, low, pivot))

    three = send(
        jnp.where(y == 0, part(3), one[edge:]),
        lambda xl, z, xh, y, core: (xl, z, xh, 3 - y, 0),
        lambda xl, z, xh, y, core: xh == 0 and core == 0 and y in (0, 1),
    )
    four = send(
        jnp.where(y == 0, part(5), two[:edge]),
        lambda xl, z, xh, y, core: (xl, z, xh, y ^ 1, 1),
        lambda xl, z, xh, y, core: xh == 0 and ((core == 0 and y == 0) or (core == 1 and y == 3)),
    )
    high = send(
        jnp.where(
            z == 0,
            jnp.where(first, layer(3), layer(1)),
            jnp.where(first, low[lift:], low[:lift]),
        ),
        lambda xl, z, xh, y, core: (xl, partner(z, core == 1), xh, y, core),
        lambda xl, z, xh, y, core: xl == 0 and z in ((0, 1) if core == 0 else (0, 3)),
    )
    five = send(part(4), lambda xl, z, xh, y, core: (xl, z, xh, y, 1), source)
    pivot = spread(pivot, 1)
    column = jnp.where(
        first,
        jnp.where(y == 0, part(0), jnp.where(y == 1, one[:edge], three)),
        jnp.where(y == 0, five, jnp.where(y == 3, two[edge:], four)),
    )
    row = jnp.where(
        z == 0,
        layer(0),
        jnp.where(
            first & (z == 1),
            low[:lift],
            jnp.where((core == 1) & (z == 3), low[lift:], high),
        ),
    )
    column, row, pivot, labels = lax.optimization_barrier((column, row, pivot, labels))

    column_across = send(
        column,
        lambda xl, z, xh, y, core: (xl, z, 1, y, core),
        lambda xl, z, xh, y, core: xh == 0,
    )
    row_across = send(
        row,
        lambda xl, z, xh, y, core: (1, z, xh, y, core),
        lambda xl, z, xh, y, core: xl == 0,
    )
    pivot = spread(pivot, 2)
    labels = lax.all_to_all(labels, AXES, 0, 0, tiled=True)
    pivot = spread(pivot, 3)
    column = jnp.where(xh == 0, column, column_across)
    row = jnp.where(xl == 0, row, row_across)
    column, row, pivot = lax.optimization_barrier((column, row, pivot))

    def around(value, step):
        return send(
            value,
            lambda xl, z, xh, y, core: (xl, z, xh, partner(y, (core == 0) == (step == 0)), core),
        )

    def along(value, step):
        return send(
            value,
            lambda xl, z, xh, y, core: (xl, partner(z, (core == 0) == (step == 0)), xh, y, core),
        )

    row_a, column_a = along(row, 0), around(column, 0)
    row_b, column_b = along(row, 1), around(column, 1)
    pivot = spread(pivot, 4)
    other = swap(column)
    pivot = spread(pivot, 5)
    column_a, row_a, pivot = lax.optimization_barrier((column_a, row_a, pivot))
    row_c, column_c = along(row_a, 1), around(column_a, 1)
    pivots = (pivot, swap(pivot))
    other_a, other_b = swap(column_a), swap(column_b)
    other_c = swap(column_c)

    def order(k, core):
        one = jnp.where(core == 0, k ^ 1, 3 - k)
        two = jnp.where(core == 0, 3 - k, k ^ 1)
        return [k, one, two, 3 - (k ^ 1)]

    pieces = [column, other, column_a, column_b, other_a, other_b, column_c, other_c]
    mine = [4 * core + k for k in order(y, core)]
    theirs = [4 * (1 - core) + k for k in order(y, 1 - core)]
    numbers = [mine[0], theirs[0], mine[1], mine[2], theirs[1], theirs[2], mine[3], theirs[3]]
    return pieces, numbers, [row, row_a, row_b, row_c], order(z, core), pivots, labels


def halves(value):
    high = value.astype(jnp.bfloat16)
    low = (value - high.astype(jnp.float32)).astype(jnp.bfloat16)
    return high, low


def dot(left, right):
    return jnp.dot(left, right, preferred_element_type=jnp.float32)


def product(left, right):
    left_high, left_low = halves(left)
    right_high, right_low = halves(right)
    return dot(left_high, right_low) + dot(left_low, right_high) + dot(left_high, right_high)


def fold_kernel(table_ref, pivot_ref, other_ref, inverse_ref, *refs):
    row_refs = refs[:4]
    high, low, right = refs[4:]
    depth = inverse_ref.shape[1]
    lift = row_refs[0].shape[0]
    for k in range(4):
        top = pl.multiple_of(table_ref[8 + k] * lift, lift)
        right[pl.ds(top, lift)] = row_refs[k][...]
    first = table_ref[14] == 0
    pivot_one = jnp.where(first, pivot_ref[...], other_ref[...])
    pivot_two = jnp.where(first, other_ref[...], pivot_ref[...])
    one = right[:depth]
    two = right[depth:] - product(pivot_two, one)
    two = product(inverse_ref[0], two)
    high[depth:], low[depth:] = halves(two)
    one = one - product(pivot_one, two)
    high[:depth], low[:depth] = halves(one)


def fold(table, pivots, inverses, layers):
    depth = inverses.shape[1]
    columns = layers[0].shape[1]
    whole = lambda *shape: pl.BlockSpec(shape, lambda i, table: (0,) * len(shape))
    half = jax.ShapeDtypeStruct((2 * depth, columns), jnp.bfloat16)
    return pl.pallas_call(
        fold_kernel,
        grid_spec=pltpu.PrefetchScalarGridSpec(
            num_scalar_prefetch=1,
            grid=(1,),
            in_specs=[
                whole(depth, depth),
                whole(depth, depth),
                pl.BlockSpec((1, depth, depth), lambda i, table: (1, 0, 0)),
            ]
            + [whole(*layers[0].shape)] * 4,
            out_specs=[whole(2 * depth, columns)] * 2,
            scratch_shapes=[pltpu.VMEM((2 * depth, columns), jnp.float32)],
        ),
        out_shape=[half, half],
        compiler_params=pltpu.CompilerParams(vmem_limit_bytes=44 * MIB),
        cost_estimate=pl.CostEstimate(
            flops=18 * depth * depth * columns, bytes_accessed=12 * MIB, transcendentals=0
        ),
        name="fold",
    )(table, *pivots, inverses, *layers)


def update_kernel(
    table_ref, owner_ref, front_ref, high, low, *refs
):
    column_refs = refs[:8]
    updated_ref, outgoing_ref, mine_ref = refs[8:11]
    held, result, held_sem, whole_sem, block_sem = refs[11:]
    step = pl.program_id(0)
    steps = pl.num_programs(0)
    slot = lax.rem(step, 2)
    tile = result.shape[1]
    edge = outgoing_ref.shape[1]
    down, across = tile // edge, result.shape[2] // edge

    def fetch(number, at):
        return pltpu.make_async_copy(column_refs[number], held.at[at], held_sem.at[at])

    def whole_copy(at, number):
        top = pl.multiple_of(table_ref[number] * tile, tile)
        return pltpu.make_async_copy(
            result.at[at], updated_ref.at[pl.ds(top, tile)], whole_sem.at[at]
        )

    def block_copies(at, number, act):
        for i in range(down):
            for j in range(across):
                owner = owner_ref[table_ref[number] * down + i, j]

                @pl.when(owner >= 0)
                def _():
                    act(
                        pltpu.make_async_copy(
                            result.at[at, pl.ds(i * edge, edge), pl.ds(j * edge, edge)],
                            outgoing_ref.at[jnp.maximum(owner, 0)],
                            block_sem.at[at],
                        )
                    )

    def finish(at, number):
        whole_copy(at, number).wait()
        block_copies(at, number, lambda copy: copy.wait())

    @pl.when(step == 0)
    def _():
        fetch(0, 0).start()

    for number in range(8):

        @pl.when(step == number)
        def _():
            if number < 7:
                fetch(number + 1, (number + 1) % 2).start()
            fetch(number, number % 2).wait()

    @pl.when(step >= 2)
    def _():
        finish(slot, step - 2)

    left = held[slot]
    left_high, left_low = halves(left)
    total = front_ref[...] - dot(left_high, low[...])
    total -= dot(left_low, high[...])
    total -= dot(left_high, high[...])
    result[slot] = total
    whole_copy(slot, step).start()
    block_copies(slot, step, lambda copy: copy.start())

    @pl.when(table_ref[step] == table_ref[12])
    def _():
        top = pl.multiple_of(table_ref[13] * edge, edge)
        mine_ref[...] = held[slot, pl.ds(top, edge)]

    @pl.when(step == steps - 1)
    def _():
        finish(1 - slot, step - 1)
        finish(slot, step)


def update(front, block_owner, high, low, pieces, table, devices, edge):
    rows, columns = front.shape
    depth = high.shape[0]
    tile = pieces[0].shape[0]
    whole = lambda *shape: pl.BlockSpec(shape, lambda i, table: (0,) * len(shape))
    return pl.pallas_call(
        update_kernel,
        grid_spec=pltpu.PrefetchScalarGridSpec(
            num_scalar_prefetch=1,
            grid=(rows // tile,),
            in_specs=[
                pl.BlockSpec(memory_space=pltpu.SMEM),
                pl.BlockSpec((tile, columns), lambda i, table: (table[i], 0)),
                whole(*high.shape),
                whole(*low.shape),
            ]
            + [pl.BlockSpec(memory_space=pl.ANY)] * 8,
            out_specs=[
                pl.BlockSpec(memory_space=pl.ANY),
                pl.BlockSpec(memory_space=pl.ANY),
                whole(edge, pieces[0].shape[1]),
            ],
            scratch_shapes=[
                pltpu.VMEM((2, tile, pieces[0].shape[1]), jnp.float32),
                pltpu.VMEM((2, tile, columns), jnp.float32),
                pltpu.SemaphoreType.DMA((2,)),
                pltpu.SemaphoreType.DMA((2,)),
                pltpu.SemaphoreType.DMA((2,)),
            ],
        ),
        out_shape=[
            jax.ShapeDtypeStruct((rows, columns), jnp.float32),
            jax.ShapeDtypeStruct((devices, edge, edge), jnp.float32),
            jax.ShapeDtypeStruct((edge, pieces[0].shape[1]), jnp.float32),
        ],
        compiler_params=pltpu.CompilerParams(vmem_limit_bytes=44 * MIB),
        cost_estimate=pl.CostEstimate(
            flops=6 * rows * columns * depth,
            bytes_accessed=40 * MIB,
            transcendentals=0,
        ),
        name="update",
    )(table, block_owner, front, high, low, *pieces)


def add_kernel(slot_ref, parent_ref, arrived_ref, out_ref, sem):
    step = pl.program_id(0)
    count = arrived_ref.shape[0]

    @pl.when(step == 0)
    def _():
        copy = pltpu.make_async_copy(parent_ref, out_ref, sem)
        copy.start()
        copy.wait()

    for k in range(count):
        slot = slot_ref[step * count + k]

        @pl.when(slot >= 0)
        def _():
            at = jnp.maximum(slot, 0)
            out_ref[at] = out_ref[at] + arrived_ref[k]


def extend_add(slots, parent, arrived):
    count = 16
    held, edge, _ = parent.shape
    return pl.pallas_call(
        add_kernel,
        grid=(arrived.shape[0] // count,),
        in_specs=[
            pl.BlockSpec(memory_space=pltpu.SMEM),
            pl.BlockSpec(memory_space=pl.ANY),
            pl.BlockSpec((count, edge, edge), lambda i: (i, 0, 0)),
        ],
        out_specs=pl.BlockSpec((held, edge, edge), lambda i: (0, 0, 0)),
        out_shape=jax.ShapeDtypeStruct(parent.shape, jnp.float32),
        scratch_shapes=[pltpu.SemaphoreType.DMA],
        compiler_params=pltpu.CompilerParams(vmem_limit_bytes=32 * MIB),
        cost_estimate=pl.CostEstimate(flops=2 * MIB, bytes_accessed=14 * MIB, transcendentals=0),
        name="extend_add",
    )(slots, parent, arrived)


def exact(left, right):
    return jnp.dot(left, right, preferred_element_type=jnp.float32, precision=lax.Precision.HIGHEST)


def local(front, inverses, block_owner, block_slot, parent_in):
    width = inverses.shape[1]
    edge = parent_in.shape[1]
    devices = lax.axis_size("row") * lax.axis_size("col")
    col = lax.axis_index("col")

    columns = front[:, : 2 * width]
    rows_one = product_rows(inverses[0], front[:width])
    rows = jnp.concatenate([rows_one, front[width : 2 * width]], axis=0)

    owners = block_owner.reshape(-1)
    slots = block_slot.reshape(-1)
    named = owners[None, :] == jnp.arange(devices, dtype=jnp.int32)[:, None]
    labels = jnp.sum(jnp.where(named, slots[None, :] + 1, 0), axis=1).astype(jnp.float32)
    pieces, numbers, layers, heights, pivots, labels = exchange(
        columns,
        rows,
        rows_one[:, width : 2 * width],
        front[width : 2 * width, :width],
        labels.reshape(devices, 1, 1),
    )
    markers = labels.reshape(devices).astype(jnp.int32) - 1
    core = col % 2
    table = jnp.stack(numbers + heights + [col // 2, col % 2, core]).astype(jnp.int32)
    high, low = fold(table, pivots, inverses, layers)
    updated, outgoing, mine = update(front, block_owner, high, low, pieces, table, devices, edge)
    arrived = lax.all_to_all(outgoing, AXES, 0, 0, tiled=True)

    mine_one, mine_two = mine[:, :width], mine[:, width:]
    corner = jnp.where(core == 0, pivots[0], pivots[1])
    mine_two = mine_two - exact(mine_one, corner)
    panels = jnp.concatenate([exact(mine_one, inverses[0]), exact(mine_two, inverses[1])], axis=1)
    parent_out = extend_add(markers, parent_in, arrived)
    return (updated, panels, parent_out)


def product_rows(left, right):
    return jnp.dot(left, right, preferred_element_type=jnp.float32, precision=lax.Precision.HIGH)


def solution(mesh):
    in_specs = (
        P("row", "col"),
        P(),
        P("row", "col"),
        P("row", "col"),
        P(("row", "col"), None, None),
    )
    out_specs = (P("row", "col"), P(("row", "col"), None), P(("row", "col"), None, None))
    return jax.shard_map(local, mesh=mesh, in_specs=in_specs, out_specs=out_specs, check_vma=False)
```

```python
import jax
import jax.numpy as jnp
from jax import lax
from jax.experimental import pallas as pl
from jax.experimental.pallas import tpu as pltpu
from jax.sharding import PartitionSpec as P

AXES = ("row", "col")
MIB = 1024 * 1024


def device(xl, z, xh, y, core):
    return (xl * 4 + z) * 16 + xh * 8 + y * 2 + core


def pairs(move, keep=lambda *place: True):
    listed = []
    for xl in range(2):
        for z in range(4):
            for xh in range(2):
                for y in range(4):
                    for core in range(2):
                        place = (xl, z, xh, y, core)
                        if keep(*place):
                            listed.append((device(*place), device(*move(*place))))
    return listed


def send(value, move, keep=lambda *place: True):
    return lax.ppermute(value, AXES, pairs(move, keep))


def place():
    row = lax.axis_index("row")
    col = lax.axis_index("col")
    return row // 4, row % 4, col // 8, (col // 2) % 4, col % 2


def partner(k, first):
    return k ^ 1 if first else 3 - k


def moved(spot, step):
    xl, z, xh, y = spot
    if step[0] == "z":
        return (xl, partner(z, step == "z0"), xh, y)
    if step[0] == "y":
        return (xl, z, xh, partner(y, step == "y0"))
    return (1 - xl, z, xh, y) if step == "xl" else (xl, z, 1 - xh, y)


def doubling():
    orders = (("xl", "xh", "z0", "z1", "y0", "y1"), ("xh", "xl", "y0", "y1", "z0", "z1"))
    having = [{(0, 0, 0, 0)}, {(0, 0, 0, 0)}]
    rounds = []
    for number in range(6):
        listed = []
        for core in range(2):
            new = {moved(spot, orders[core][number]): spot for spot in sorted(having[core])}
            for to, start in new.items():
                listed.append((device(*start, core), device(*to, core)))
            having[core] = having[core] | set(new)
        rounds.append(listed)
    return rounds


def exchange(columns, make_rows, labels):
    xl, z, xh, y, core = place()
    first = core == 0
    edge = columns.shape[0] // 8
    lift = columns.shape[1] // 4
    part = lambda k, count=1: columns[k * edge : (k + count) * edge]
    layer = lambda k, count=1: rows[k * lift : (k + count) * lift]
    rounds = doubling()
    corner = ((xl == 0) & (z == 0)) & ((xh == 0) & (y == 0))

    def swap(value):
        return send(value, lambda xl, z, xh, y, core: (xl, z, xh, y, 1 - core))

    def spread(value, number):
        return value + lax.ppermute(value, AXES, rounds[number])

    source = lambda xl, z, xh, y, core: xh == 0 and y == 0 and core == 0

    half = columns.shape[1] // 2
    beside = lax.ppermute(columns[half : 2 * half, :half], AXES, [(0, 1)])

    one = send(part(1, 2), lambda xl, z, xh, y, core: (xl, z, xh, 1, 0), source)
    two = send(part(6, 2), lambda xl, z, xh, y, core: (xl, z, xh, 3, 1), source)
    rows = make_rows()
    low = send(
        jnp.where(first, layer(1, 2), layer(2, 2)),
        lambda xl, z, xh, y, core: (xl, partner(z, core == 0), xh, y, core),
        lambda xl, z, xh, y, core: xl == 0 and z == 0,
    )
    pivot = jnp.where(corner & first, rows[:half, half:], beside)
    pivot = spread(pivot, 0)
    one, two, low, pivot, columns, rows = lax.optimization_barrier(
        (one, two, low, pivot, columns, rows)
    )

    three = send(
        jnp.where(y == 0, part(3), one[edge:]),
        lambda xl, z, xh, y, core: (xl, z, xh, 3 - y, 0),
        lambda xl, z, xh, y, core: xh == 0 and core == 0 and y in (0, 1),
    )
    four = send(
        jnp.where(y == 0, part(5), two[:edge]),
        lambda xl, z, xh, y, core: (xl, z, xh, y ^ 1, 1),
        lambda xl, z, xh, y, core: xh == 0 and ((core == 0 and y == 0) or (core == 1 and y == 3)),
    )
    high = send(
        jnp.where(
            z == 0,
            jnp.where(first, layer(3), layer(1)),
            jnp.where(first, low[lift:], low[:lift]),
        ),
        lambda xl, z, xh, y, core: (xl, partner(z, core == 1), xh, y, core),
        lambda xl, z, xh, y, core: xl == 0 and z in ((0, 1) if core == 0 else (0, 3)),
    )
    five = send(part(4), lambda xl, z, xh, y, core: (xl, z, xh, y, 1), source)
    pivot = spread(pivot, 1)
    column = jnp.where(
        first,
        jnp.where(y == 0, part(0), jnp.where(y == 1, one[:edge], three)),
        jnp.where(y == 0, five, jnp.where(y == 3, two[edge:], four)),
    )
    row = jnp.where(
        z == 0,
        layer(0),
        jnp.where(
            first & (z == 1),
            low[:lift],
            jnp.where((core == 1) & (z == 3), low[lift:], high),
        ),
    )
    column, row, pivot, labels = lax.optimization_barrier((column, row, pivot, labels))

    column_across = send(
        column,
        lambda xl, z, xh, y, core: (xl, z, 1, y, core),
        lambda xl, z, xh, y, core: xh == 0,
    )
    row_across = send(
        row,
        lambda xl, z, xh, y, core: (1, z, xh, y, core),
        lambda xl, z, xh, y, core: xl == 0,
    )
    pivot = spread(pivot, 2)
    labels = lax.all_to_all(labels, AXES, 0, 0, tiled=True)
    pivot = spread(pivot, 3)
    pivot = spread(pivot, 4)
    column = jnp.where(xh == 0, column, column_across)
    row = jnp.where(xl == 0, row, row_across)
    column, row, pivot, labels = lax.optimization_barrier((column, row, pivot, labels))

    def around(value, step):
        return send(
            value,
            lambda xl, z, xh, y, core: (xl, z, xh, partner(y, (core == 0) == (step == 0)), core),
        )

    def along(value, step):
        return send(
            value,
            lambda xl, z, xh, y, core: (xl, partner(z, (core == 0) == (step == 0)), xh, y, core),
        )

    row_a, column_a = along(row, 0), around(column, 0)
    row_b, column_b = along(row, 1), around(column, 1)
    other = swap(column)
    pivot = spread(pivot, 5)
    column_a, row_a, pivot = lax.optimization_barrier((column_a, row_a, pivot))
    row_c, column_c = along(row_a, 1), around(column_a, 1)
    pivots = (pivot, swap(pivot))
    other_a, other_b = swap(column_a), swap(column_b)
    other_c = swap(column_c)

    def order(k, core):
        one = jnp.where(core == 0, k ^ 1, 3 - k)
        two = jnp.where(core == 0, 3 - k, k ^ 1)
        return [k, one, two, 3 - (k ^ 1)]

    pieces = [column, other, column_a, column_b, other_a, other_b, column_c, other_c]
    mine = [4 * core + k for k in order(y, core)]
    theirs = [4 * (1 - core) + k for k in order(y, 1 - core)]
    numbers = [mine[0], theirs[0], mine[1], mine[2], theirs[1], theirs[2], mine[3], theirs[3]]
    return pieces, numbers, [row, row_a, row_b, row_c], order(z, core), pivots, labels


def halves(value):
    high = value.astype(jnp.bfloat16)
    low = (value - high.astype(jnp.float32)).astype(jnp.bfloat16)
    return high, low


def dot(left, right):
    return jnp.dot(left, right, preferred_element_type=jnp.float32)


def product(left, right):
    left_high, left_low = halves(left)
    right_high, right_low = halves(right)
    return dot(left_high, right_low) + dot(left_low, right_high) + dot(left_high, right_high)


def fold_kernel(table_ref, pivot_ref, other_ref, inverse_ref, *refs):
    row_refs = refs[:4]
    high, low, right = refs[4:]
    depth = inverse_ref.shape[1]
    lift = row_refs[0].shape[0]
    for k in range(4):
        top = pl.multiple_of(table_ref[8 + k] * lift, lift)
        right[pl.ds(top, lift)] = row_refs[k][...]
    first = table_ref[14] == 0
    pivot_one = jnp.where(first, pivot_ref[...], other_ref[...])
    pivot_two = jnp.where(first, other_ref[...], pivot_ref[...])
    one = right[:depth]
    two = right[depth:] - product(pivot_two, one)
    two = product(inverse_ref[0], two)
    high[depth:], low[depth:] = halves(two)
    one = one - product(pivot_one, two)
    high[:depth], low[:depth] = halves(one)


def fold(table, pivots, inverses, layers):
    depth = inverses.shape[1]
    columns = layers[0].shape[1]
    whole = lambda *shape: pl.BlockSpec(shape, lambda i, table: (0,) * len(shape))
    half = jax.ShapeDtypeStruct((2 * depth, columns), jnp.bfloat16)
    return pl.pallas_call(
        fold_kernel,
        grid_spec=pltpu.PrefetchScalarGridSpec(
            num_scalar_prefetch=1,
            grid=(1,),
            in_specs=[
                whole(depth, depth),
                whole(depth, depth),
                pl.BlockSpec((1, depth, depth), lambda i, table: (1, 0, 0)),
            ]
            + [whole(*layers[0].shape)] * 4,
            out_specs=[whole(2 * depth, columns)] * 2,
            scratch_shapes=[pltpu.VMEM((2 * depth, columns), jnp.float32)],
        ),
        out_shape=[half, half],
        compiler_params=pltpu.CompilerParams(vmem_limit_bytes=36 * MIB),
        cost_estimate=pl.CostEstimate(
            flops=18 * depth * depth * columns, bytes_accessed=12 * MIB, transcendentals=0
        ),
        name="fold",
    )(table, *pivots, inverses, *layers)


def update_kernel(
    table_ref, owner_ref, front_ref, high, low, *refs
):
    column_refs = refs[:8]
    updated_ref, outgoing_ref, mine_ref = refs[8:11]
    held, result, held_sem, whole_sem, block_sem = refs[11:]
    step = pl.program_id(0)
    steps = pl.num_programs(0)
    slot = lax.rem(step, 2)
    tile = result.shape[1]
    edge = outgoing_ref.shape[1]
    down, across = tile // edge, result.shape[2] // edge

    def fetch(number, at):
        return pltpu.make_async_copy(column_refs[number], held.at[at], held_sem.at[at])

    def whole_copy(at, number):
        top = pl.multiple_of(table_ref[number] * tile, tile)
        return pltpu.make_async_copy(
            result.at[at], updated_ref.at[pl.ds(top, tile)], whole_sem.at[at]
        )

    def block_copies(at, number, act):
        for i in range(down):
            for j in range(across):
                owner = owner_ref[table_ref[number] * down + i, j]

                @pl.when(owner >= 0)
                def _():
                    act(
                        pltpu.make_async_copy(
                            result.at[at, pl.ds(i * edge, edge), pl.ds(j * edge, edge)],
                            outgoing_ref.at[jnp.maximum(owner, 0)],
                            block_sem.at[at],
                        )
                    )

    def finish(at, number):
        whole_copy(at, number).wait()
        block_copies(at, number, lambda copy: copy.wait())

    @pl.when(step == 0)
    def _():
        fetch(0, 0).start()

    for number in range(8):

        @pl.when(step == number)
        def _():
            if number < 7:
                fetch(number + 1, (number + 1) % 2).start()
            fetch(number, number % 2).wait()

    @pl.when(step >= 2)
    def _():
        finish(slot, step - 2)

    left = held[slot]
    left_high, left_low = halves(left)
    total = front_ref[...] - dot(left_high, low[...])
    total -= dot(left_low, high[...])
    total -= dot(left_high, high[...])
    result[slot] = total
    whole_copy(slot, step).start()
    block_copies(slot, step, lambda copy: copy.start())

    @pl.when(table_ref[step] == table_ref[12])
    def _():
        top = pl.multiple_of(table_ref[13] * edge, edge)
        mine_ref[...] = held[slot, pl.ds(top, edge)]

    @pl.when(step == steps - 1)
    def _():
        finish(1 - slot, step - 1)
        finish(slot, step)


def update(front, block_owner, high, low, pieces, table, devices, edge):
    rows, columns = front.shape
    depth = high.shape[0]
    tile = pieces[0].shape[0]
    whole = lambda *shape: pl.BlockSpec(shape, lambda i, table: (0,) * len(shape))
    return pl.pallas_call(
        update_kernel,
        grid_spec=pltpu.PrefetchScalarGridSpec(
            num_scalar_prefetch=1,
            grid=(rows // tile,),
            in_specs=[
                pl.BlockSpec(memory_space=pltpu.SMEM),
                pl.BlockSpec((tile, columns), lambda i, table: (table[i], 0)),
                whole(*high.shape),
                whole(*low.shape),
            ]
            + [pl.BlockSpec(memory_space=pl.ANY)] * 8,
            out_specs=[
                pl.BlockSpec(memory_space=pl.ANY),
                pl.BlockSpec(memory_space=pl.ANY),
                whole(edge, pieces[0].shape[1]),
            ],
            scratch_shapes=[
                pltpu.VMEM((2, tile, pieces[0].shape[1]), jnp.float32),
                pltpu.VMEM((2, tile, columns), jnp.float32),
                pltpu.SemaphoreType.DMA((2,)),
                pltpu.SemaphoreType.DMA((2,)),
                pltpu.SemaphoreType.DMA((2,)),
            ],
        ),
        out_shape=[
            jax.ShapeDtypeStruct((rows, columns), jnp.float32),
            jax.ShapeDtypeStruct((devices, edge, edge), jnp.float32),
            jax.ShapeDtypeStruct((edge, pieces[0].shape[1]), jnp.float32),
        ],
        compiler_params=pltpu.CompilerParams(vmem_limit_bytes=28 * MIB),
        cost_estimate=pl.CostEstimate(
            flops=6 * rows * columns * depth,
            bytes_accessed=40 * MIB,
            transcendentals=0,
        ),
        name="update",
    )(table, block_owner, front, high, low, *pieces)


def add_kernel(slot_ref, parent_ref, arrived_ref, out_ref, sem):
    step = pl.program_id(0)
    count = arrived_ref.shape[0]

    @pl.when(step == 0)
    def _():
        copy = pltpu.make_async_copy(parent_ref, out_ref, sem)
        copy.start()
        copy.wait()

    for k in range(count):
        slot = slot_ref[step * count + k]

        @pl.when(slot >= 0)
        def _():
            at = jnp.maximum(slot, 0)
            out_ref[at] = out_ref[at] + arrived_ref[k]


def extend_add(slots, parent, arrived):
    count = 16
    held, edge, _ = parent.shape
    return pl.pallas_call(
        add_kernel,
        grid=(arrived.shape[0] // count,),
        in_specs=[
            pl.BlockSpec(memory_space=pltpu.SMEM),
            pl.BlockSpec(memory_space=pl.ANY),
            pl.BlockSpec((count, edge, edge), lambda i: (i, 0, 0)),
        ],
        out_specs=pl.BlockSpec((held, edge, edge), lambda i: (0, 0, 0)),
        out_shape=jax.ShapeDtypeStruct(parent.shape, jnp.float32),
        scratch_shapes=[pltpu.SemaphoreType.DMA],
        compiler_params=pltpu.CompilerParams(vmem_limit_bytes=32 * MIB),
        cost_estimate=pl.CostEstimate(flops=2 * MIB, bytes_accessed=14 * MIB, transcendentals=0),
        name="extend_add",
    )(slots, parent, arrived)


def exact(left, right):
    return jnp.dot(left, right, preferred_element_type=jnp.float32, precision=lax.Precision.HIGHEST)


def local(front, inverses, block_owner, block_slot, parent_in):
    width = inverses.shape[1]
    edge = parent_in.shape[1]
    devices = lax.axis_size("row") * lax.axis_size("col")
    col = lax.axis_index("col")

    columns = front[:, : 2 * width]

    def make_rows():
        return jnp.concatenate(
            [product_rows(inverses[0], front[:width]), front[width : 2 * width]], axis=0
        )

    owners = block_owner.reshape(-1)
    slots = block_slot.reshape(-1)
    named = owners[None, :] == jnp.arange(devices, dtype=jnp.int32)[:, None]
    labels = jnp.sum(jnp.where(named, slots[None, :] + 1, 0), axis=1).astype(jnp.float32)
    pieces, numbers, layers, heights, pivots, labels = exchange(
        columns, make_rows, labels.reshape(devices, 1, 1)
    )
    markers = labels.reshape(devices).astype(jnp.int32) - 1
    core = col % 2
    table = jnp.stack(numbers + heights + [col // 2, col % 2, core]).astype(jnp.int32)
    high, low = fold(table, pivots, inverses, layers)
    updated, outgoing, mine = update(front, block_owner, high, low, pieces, table, devices, edge)
    arrived = lax.all_to_all(outgoing, AXES, 0, 0, tiled=True)

    mine_one, mine_two = mine[:, :width], mine[:, width:]
    corner = jnp.where(core == 0, pivots[0], pivots[1])
    mine_two = mine_two - exact(mine_one, corner)
    panels = jnp.concatenate([exact(mine_one, inverses[0]), exact(mine_two, inverses[1])], axis=1)
    parent_out = extend_add(markers, parent_in, arrived)
    return (updated, panels, parent_out)


def product_rows(left, right):
    return jnp.dot(left, right, preferred_element_type=jnp.float32, precision=lax.Precision.HIGH)


def solution(mesh):
    in_specs = (
        P("row", "col"),
        P(),
        P("row", "col"),
        P("row", "col"),
        P(("row", "col"), None, None),
    )
    out_specs = (P("row", "col"), P(("row", "col"), None), P(("row", "col"), None, None))
    return jax.shard_map(local, mesh=mesh, in_specs=in_specs, out_specs=out_specs, check_vma=False)
```

```python
import jax
import jax.numpy as jnp
from jax import lax
from jax.experimental import pallas as pl
from jax.experimental.pallas import tpu as pltpu
from jax.sharding import PartitionSpec as P

AXES = ("row", "col")
MIB = 1024 * 1024


def device(xl, z, xh, y, core):
    return (xl * 4 + z) * 16 + xh * 8 + y * 2 + core


def pairs(move, keep=lambda *place: True):
    listed = []
    for xl in range(2):
        for z in range(4):
            for xh in range(2):
                for y in range(4):
                    for core in range(2):
                        place = (xl, z, xh, y, core)
                        if keep(*place):
                            listed.append((device(*place), device(*move(*place))))
    return listed


def send(value, move, keep=lambda *place: True):
    return lax.ppermute(value, AXES, pairs(move, keep))


def place():
    row = lax.axis_index("row")
    col = lax.axis_index("col")
    return row // 4, row % 4, col // 8, (col // 2) % 4, col % 2


def partner(k, first):
    return k ^ 1 if first else 3 - k


def moved(spot, step):
    xl, z, xh, y = spot
    if step[0] == "z":
        return (xl, partner(z, step == "z0"), xh, y)
    if step[0] == "y":
        return (xl, z, xh, partner(y, step == "y0"))
    return (1 - xl, z, xh, y) if step == "xl" else (xl, z, 1 - xh, y)


def doubling():
    orders = (("xl", "xh", "z0", "z1", "y0", "y1"), ("xh", "xl", "y0", "y1", "z0", "z1"))
    having = [{(0, 0, 0, 0)}, {(0, 0, 0, 0)}]
    rounds = []
    for number in range(6):
        listed = []
        for core in range(2):
            new = {moved(spot, orders[core][number]): spot for spot in sorted(having[core])}
            for to, start in new.items():
                listed.append((device(*start, core), device(*to, core)))
            having[core] = having[core] | set(new)
        rounds.append(listed)
    return rounds


def exchange(front, columns, make_rows, labels):
    xl, z, xh, y, core = place()
    first = core == 0
    edge = columns.shape[0] // 8
    lift = columns.shape[1] // 4
    part = lambda k, count=1: columns[k * edge : (k + count) * edge]
    layer = lambda k, count=1: rows[k * lift : (k + count) * lift]
    rounds = doubling()
    corner = ((xl == 0) & (z == 0)) & ((xh == 0) & (y == 0))

    def swap(value):
        return send(value, lambda xl, z, xh, y, core: (xl, z, xh, y, 1 - core))

    def spread(value, number):
        return value + lax.ppermute(value, AXES, rounds[number])

    source = lambda xl, z, xh, y, core: xh == 0 and y == 0 and core == 0

    half = columns.shape[1] // 2
    beside = lax.ppermute(columns[half : 2 * half, :half], AXES, [(0, 1)])

    one = send(part(1, 2), lambda xl, z, xh, y, core: (xl, z, xh, 1, 0), source)
    two = send(part(6, 2), lambda xl, z, xh, y, core: (xl, z, xh, 3, 1), source)
    beside, front = lax.optimization_barrier((beside, front))
    rows = make_rows(front)
    low = send(
        jnp.where(first, layer(1, 2), layer(2, 2)),
        lambda xl, z, xh, y, core: (xl, partner(z, core == 0), xh, y, core),
        lambda xl, z, xh, y, core: xl == 0 and z == 0,
    )
    pivot = jnp.where(corner & first, rows[:half, half:], beside)
    pivot = spread(pivot, 0)
    one, two, low, columns, rows = lax.optimization_barrier((one, two, low, columns, rows))

    three = send(
        jnp.where(y == 0, part(3), one[edge:]),
        lambda xl, z, xh, y, core: (xl, z, xh, 3 - y, 0),
        lambda xl, z, xh, y, core: xh == 0 and core == 0 and y in (0, 1),
    )
    four = send(
        jnp.where(y == 0, part(5), two[:edge]),
        lambda xl, z, xh, y, core: (xl, z, xh, y ^ 1, 1),
        lambda xl, z, xh, y, core: xh == 0 and ((core == 0 and y == 0) or (core == 1 and y == 3)),
    )
    high = send(
        jnp.where(
            z == 0,
            jnp.where(first, layer(3), layer(1)),
            jnp.where(first, low[lift:], low[:lift]),
        ),
        lambda xl, z, xh, y, core: (xl, partner(z, core == 1), xh, y, core),
        lambda xl, z, xh, y, core: xl == 0 and z in ((0, 1) if core == 0 else (0, 3)),
    )
    five = send(part(4), lambda xl, z, xh, y, core: (xl, z, xh, y, 1), source)
    pivot = spread(pivot, 1)
    column = jnp.where(
        first,
        jnp.where(y == 0, part(0), jnp.where(y == 1, one[:edge], three)),
        jnp.where(y == 0, five, jnp.where(y == 3, two[edge:], four)),
    )
    row = jnp.where(
        z == 0,
        layer(0),
        jnp.where(
            first & (z == 1),
            low[:lift],
            jnp.where((core == 1) & (z == 3), low[lift:], high),
        ),
    )
    column, row, labels = lax.optimization_barrier((column, row, labels))

    column_across = send(
        column,
        lambda xl, z, xh, y, core: (xl, z, 1, y, core),
        lambda xl, z, xh, y, core: xh == 0,
    )
    row_across = send(
        row,
        lambda xl, z, xh, y, core: (1, z, xh, y, core),
        lambda xl, z, xh, y, core: xl == 0,
    )
    pivot = spread(pivot, 2)
    labels = lax.all_to_all(labels, AXES, 0, 0, tiled=True)
    pivot = spread(pivot, 3)
    pivot = spread(pivot, 4)
    column = jnp.where(xh == 0, column, column_across)
    row = jnp.where(xl == 0, row, row_across)
    column, row, pivot, labels = lax.optimization_barrier((column, row, pivot, labels))

    def around(value, step):
        return send(
            value,
            lambda xl, z, xh, y, core: (xl, z, xh, partner(y, (core == 0) == (step == 0)), core),
        )

    def along(value, step):
        return send(
            value,
            lambda xl, z, xh, y, core: (xl, partner(z, (core == 0) == (step == 0)), xh, y, core),
        )

    row_a, column_a = along(row, 0), around(column, 0)
    row_b, column_b = along(row, 1), around(column, 1)
    other = swap(column)
    pivot = spread(pivot, 5)
    column_a, row_a = lax.optimization_barrier((column_a, row_a))
    row_c, column_c = along(row_a, 1), around(column_a, 1)
    pivots = (pivot, swap(pivot))
    other_a, other_b = swap(column_a), swap(column_b)
    other_c = swap(column_c)

    def order(k, core):
        one = jnp.where(core == 0, k ^ 1, 3 - k)
        two = jnp.where(core == 0, 3 - k, k ^ 1)
        return [k, one, two, 3 - (k ^ 1)]

    pieces = [column, other, column_a, column_b, other_a, other_b, column_c, other_c]
    mine = [4 * core + k for k in order(y, core)]
    theirs = [4 * (1 - core) + k for k in order(y, 1 - core)]
    numbers = [mine[0], theirs[0], mine[1], mine[2], theirs[1], theirs[2], mine[3], theirs[3]]
    return pieces, numbers, [row, row_a, row_b, row_c], order(z, core), pivots, labels


def halves(value):
    high = value.astype(jnp.bfloat16)
    low = (value - high.astype(jnp.float32)).astype(jnp.bfloat16)
    return high, low


def dot(left, right):
    return jnp.dot(left, right, preferred_element_type=jnp.float32)


def product(left, right):
    left_high, left_low = halves(left)
    right_high, right_low = halves(right)
    return dot(left_high, right_low) + dot(left_low, right_high) + dot(left_high, right_high)


def update_kernel(
    table_ref, owner_ref, front_ref, pivot_ref, other_ref, inverse_ref, *refs
):
    column_refs = refs[:8]
    row_refs = refs[8:12]
    updated_ref, outgoing_ref, mine_ref = refs[12:15]
    right, high, low, held, result, held_sem, whole_sem, block_sem = refs[15:]
    depth = inverse_ref.shape[1]
    step = pl.program_id(0)
    steps = pl.num_programs(0)
    slot = lax.rem(step, 2)
    tile = result.shape[1]
    edge = outgoing_ref.shape[1]
    down, across = tile // edge, result.shape[2] // edge

    def fetch(number, at):
        return pltpu.make_async_copy(column_refs[number], held.at[at], held_sem.at[at])

    def whole_copy(at, number):
        top = pl.multiple_of(table_ref[number] * tile, tile)
        return pltpu.make_async_copy(
            result.at[at], updated_ref.at[pl.ds(top, tile)], whole_sem.at[at]
        )

    def block_copies(at, number, act):
        for i in range(down):
            for j in range(across):
                owner = owner_ref[table_ref[number] * down + i, j]

                @pl.when(owner >= 0)
                def _():
                    act(
                        pltpu.make_async_copy(
                            result.at[at, pl.ds(i * edge, edge), pl.ds(j * edge, edge)],
                            outgoing_ref.at[jnp.maximum(owner, 0)],
                            block_sem.at[at],
                        )
                    )

    def finish(at, number):
        whole_copy(at, number).wait()
        block_copies(at, number, lambda copy: copy.wait())

    @pl.when(step == 0)
    def _():
        fetch(0, 0).start()
        lift = row_refs[0].shape[0]
        for k in range(4):
            top = pl.multiple_of(table_ref[8 + k] * lift, lift)
            right[pl.ds(top, lift)] = row_refs[k][...]
        first = table_ref[14] == 0
        pivot_one = jnp.where(first, pivot_ref[...], other_ref[...])
        pivot_two = jnp.where(first, other_ref[...], pivot_ref[...])
        one = right[:depth]
        two = right[depth:] - product(pivot_two, one)
        two = product(inverse_ref[0], two)
        high[depth:], low[depth:] = halves(two)
        one = one - product(pivot_one, two)
        high[:depth], low[:depth] = halves(one)

    for number in range(8):

        @pl.when(step == number)
        def _():
            if number < 7:
                fetch(number + 1, (number + 1) % 2).start()
            fetch(number, number % 2).wait()

    @pl.when(step >= 2)
    def _():
        finish(slot, step - 2)

    left = held[slot]
    left_high, left_low = halves(left)
    total = front_ref[...] - dot(left_high, low[...])
    total -= dot(left_low, high[...])
    total -= dot(left_high, high[...])
    result[slot] = total
    whole_copy(slot, step).start()
    block_copies(slot, step, lambda copy: copy.start())

    @pl.when(table_ref[step] == table_ref[12])
    def _():
        top = pl.multiple_of(table_ref[13] * edge, edge)
        mine_ref[...] = held[slot, pl.ds(top, edge)]

    @pl.when(step == steps - 1)
    def _():
        finish(1 - slot, step - 1)
        finish(slot, step)


def update(front, block_owner, pivots, inverses, pieces, layers, table, devices, edge):
    rows, columns = front.shape
    depth = inverses.shape[1]
    tile = pieces[0].shape[0]
    whole = lambda *shape: pl.BlockSpec(shape, lambda i, table: (0,) * len(shape))
    return pl.pallas_call(
        update_kernel,
        grid_spec=pltpu.PrefetchScalarGridSpec(
            num_scalar_prefetch=1,
            grid=(rows // tile,),
            in_specs=[
                pl.BlockSpec(memory_space=pltpu.SMEM),
                pl.BlockSpec((tile, columns), lambda i, table: (table[i], 0)),
                whole(depth, depth),
                whole(depth, depth),
                pl.BlockSpec((1, depth, depth), lambda i, table: (1, 0, 0)),
            ]
            + [pl.BlockSpec(memory_space=pl.ANY)] * 8
            + [whole(*layers[0].shape)] * 4,
            out_specs=[
                pl.BlockSpec(memory_space=pl.ANY),
                pl.BlockSpec(memory_space=pl.ANY),
                whole(edge, pieces[0].shape[1]),
            ],
            scratch_shapes=[
                pltpu.VMEM((2 * depth, columns), jnp.float32),
                pltpu.VMEM((2 * depth, columns), jnp.bfloat16),
                pltpu.VMEM((2 * depth, columns), jnp.bfloat16),
                pltpu.VMEM((2, tile, pieces[0].shape[1]), jnp.float32),
                pltpu.VMEM((2, tile, columns), jnp.float32),
                pltpu.SemaphoreType.DMA((2,)),
                pltpu.SemaphoreType.DMA((2,)),
                pltpu.SemaphoreType.DMA((2,)),
            ],
        ),
        out_shape=[
            jax.ShapeDtypeStruct((rows, columns), jnp.float32),
            jax.ShapeDtypeStruct((devices, edge, edge), jnp.float32),
            jax.ShapeDtypeStruct((edge, pieces[0].shape[1]), jnp.float32),
        ],
        compiler_params=pltpu.CompilerParams(vmem_limit_bytes=46 * MIB),
        cost_estimate=pl.CostEstimate(
            flops=16 * rows * columns * depth,
            bytes_accessed=40 * MIB,
            transcendentals=0,
        ),
        name="update",
    )(table, block_owner, front, *pivots, inverses, *pieces, *layers)


def add_kernel(slot_ref, parent_ref, arrived_ref, out_ref, sem):
    step = pl.program_id(0)
    count = arrived_ref.shape[0]

    @pl.when(step == 0)
    def _():
        copy = pltpu.make_async_copy(parent_ref, out_ref, sem)
        copy.start()
        copy.wait()

    for k in range(count):
        slot = slot_ref[step * count + k]

        @pl.when(slot >= 0)
        def _():
            at = jnp.maximum(slot, 0)
            out_ref[at] = out_ref[at] + arrived_ref[k]


def extend_add(slots, parent, arrived):
    count = 16
    held, edge, _ = parent.shape
    return pl.pallas_call(
        add_kernel,
        grid=(arrived.shape[0] // count,),
        in_specs=[
            pl.BlockSpec(memory_space=pltpu.SMEM),
            pl.BlockSpec(memory_space=pl.ANY),
            pl.BlockSpec((count, edge, edge), lambda i: (i, 0, 0)),
        ],
        out_specs=pl.BlockSpec((held, edge, edge), lambda i: (0, 0, 0)),
        out_shape=jax.ShapeDtypeStruct(parent.shape, jnp.float32),
        scratch_shapes=[pltpu.SemaphoreType.DMA],
        compiler_params=pltpu.CompilerParams(vmem_limit_bytes=32 * MIB),
        cost_estimate=pl.CostEstimate(flops=2 * MIB, bytes_accessed=14 * MIB, transcendentals=0),
        name="extend_add",
    )(slots, parent, arrived)


def exact(left, right):
    return jnp.dot(left, right, preferred_element_type=jnp.float32, precision=lax.Precision.HIGHEST)


def local(front, inverses, block_owner, block_slot, parent_in):
    width = inverses.shape[1]
    edge = parent_in.shape[1]
    devices = lax.axis_size("row") * lax.axis_size("col")
    col = lax.axis_index("col")

    columns = front[:, : 2 * width]

    def make_rows(front):
        return jnp.concatenate(
            [product_rows(inverses[0], front[:width]), front[width : 2 * width]], axis=0
        )

    owners = block_owner.reshape(-1)
    slots = block_slot.reshape(-1)
    named = owners[None, :] == jnp.arange(devices, dtype=jnp.int32)[:, None]
    labels = jnp.sum(jnp.where(named, slots[None, :] + 1, 0), axis=1).astype(jnp.float32)
    pieces, numbers, layers, heights, pivots, labels = exchange(
        front[: 2 * width], columns, make_rows, labels.reshape(devices, 1, 1)
    )
    markers = labels.reshape(devices).astype(jnp.int32) - 1
    core = col % 2
    table = jnp.stack(numbers + heights + [col // 2, col % 2, core]).astype(jnp.int32)
    updated, outgoing, mine = update(
        front, block_owner, pivots, inverses, pieces, layers, table, devices, edge
    )
    arrived = lax.all_to_all(outgoing, AXES, 0, 0, tiled=True)

    mine_one, mine_two = mine[:, :width], mine[:, width:]
    corner = jnp.where(core == 0, pivots[0], pivots[1])
    mine_two = mine_two - exact(mine_one, corner)
    panels = jnp.concatenate([exact(mine_one, inverses[0]), exact(mine_two, inverses[1])], axis=1)
    parent_out = extend_add(markers, parent_in, arrived)
    return (updated, panels, parent_out)


def product_rows(left, right):
    return jnp.dot(left, right, preferred_element_type=jnp.float32, precision=lax.Precision.HIGH)


def solution(mesh):
    in_specs = (
        P("row", "col"),
        P(),
        P("row", "col"),
        P("row", "col"),
        P(("row", "col"), None, None),
    )
    out_specs = (P("row", "col"), P(("row", "col"), None), P(("row", "col"), None, None))
    return jax.shard_map(local, mesh=mesh, in_specs=in_specs, out_specs=out_specs, check_vma=False)
```

```python
import jax
import jax.numpy as jnp
from jax import lax
from jax.experimental import pallas as pl
from jax.experimental.pallas import tpu as pltpu
from jax.sharding import PartitionSpec as P

AXES = ("row", "col")
MIB = 1024 * 1024


def device(xl, z, xh, y, core):
    return (xl * 4 + z) * 16 + xh * 8 + y * 2 + core


def pairs(move, keep=lambda *place: True):
    listed = []
    for xl in range(2):
        for z in range(4):
            for xh in range(2):
                for y in range(4):
                    for core in range(2):
                        place = (xl, z, xh, y, core)
                        if keep(*place):
                            listed.append((device(*place), device(*move(*place))))
    return listed


def send(value, move, keep=lambda *place: True):
    return lax.ppermute(value, AXES, pairs(move, keep))


def place():
    row = lax.axis_index("row")
    col = lax.axis_index("col")
    return row // 4, row % 4, col // 8, (col // 2) % 4, col % 2


def partner(k, first):
    return k ^ 1 if first else 3 - k


def moved(spot, step):
    xl, z, xh, y = spot
    if step[0] == "z":
        return (xl, partner(z, step == "z0"), xh, y)
    if step[0] == "y":
        return (xl, z, xh, partner(y, step == "y0"))
    return (1 - xl, z, xh, y) if step == "xl" else (xl, z, 1 - xh, y)


def doubling():
    orders = (("xl", "xh", "z0", "z1", "y0", "y1"), ("xh", "xl", "y0", "y1", "z0", "z1"))
    having = [{(0, 0, 0, 0)}, {(0, 0, 0, 0)}]
    rounds = []
    for number in range(6):
        listed = []
        for core in range(2):
            new = {moved(spot, orders[core][number]): spot for spot in sorted(having[core])}
            for to, start in new.items():
                listed.append((device(*start, core), device(*to, core)))
            having[core] = having[core] | set(new)
        rounds.append(listed)
    return rounds


def exchange(front, columns, make_rows, labels):
    xl, z, xh, y, core = place()
    first = core == 0
    edge = columns.shape[0] // 8
    lift = columns.shape[1] // 4
    part = lambda k, count=1: columns[k * edge : (k + count) * edge]
    layer = lambda k, count=1: rows[k * lift : (k + count) * lift]
    rounds = doubling()
    corner = ((xl == 0) & (z == 0)) & ((xh == 0) & (y == 0))

    def swap(value):
        return send(value, lambda xl, z, xh, y, core: (xl, z, xh, y, 1 - core))

    def spread(value, number):
        return value + lax.ppermute(value, AXES, rounds[number])

    source = lambda xl, z, xh, y, core: xh == 0 and y == 0 and core == 0

    half = columns.shape[1] // 2
    beside = lax.ppermute(columns[half : 2 * half, :half], AXES, [(0, 1)])

    one = send(part(1, 2), lambda xl, z, xh, y, core: (xl, z, xh, 1, 0), source)
    two = send(part(6, 2), lambda xl, z, xh, y, core: (xl, z, xh, 3, 1), source)
    beside, front = lax.optimization_barrier((beside, front))
    rows = make_rows(front)
    low = send(
        jnp.where(first, layer(1, 2), layer(2, 2)),
        lambda xl, z, xh, y, core: (xl, partner(z, core == 0), xh, y, core),
        lambda xl, z, xh, y, core: xl == 0 and z == 0,
    )
    pivot = jnp.where(corner & first, rows[:half, half:], beside)
    pivot = spread(pivot, 0)
    one, two, low, pivot, columns, rows = lax.optimization_barrier(
        (one, two, low, pivot, columns, rows)
    )

    three = send(
        jnp.where(y == 0, part(3), one[edge:]),
        lambda xl, z, xh, y, core: (xl, z, xh, 3 - y, 0),
        lambda xl, z, xh, y, core: xh == 0 and core == 0 and y in (0, 1),
    )
    four = send(
        jnp.where(y == 0, part(5), two[:edge]),
        lambda xl, z, xh, y, core: (xl, z, xh, y ^ 1, 1),
        lambda xl, z, xh, y, core: xh == 0 and ((core == 0 and y == 0) or (core == 1 and y == 3)),
    )
    high = send(
        jnp.where(
            z == 0,
            jnp.where(first, layer(3), layer(1)),
            jnp.where(first, low[lift:], low[:lift]),
        ),
        lambda xl, z, xh, y, core: (xl, partner(z, core == 1), xh, y, core),
        lambda xl, z, xh, y, core: xl == 0 and z in ((0, 1) if core == 0 else (0, 3)),
    )
    five = send(part(4), lambda xl, z, xh, y, core: (xl, z, xh, y, 1), source)
    pivot = spread(pivot, 1)
    column = jnp.where(
        first,
        jnp.where(y == 0, part(0), jnp.where(y == 1, one[:edge], three)),
        jnp.where(y == 0, five, jnp.where(y == 3, two[edge:], four)),
    )
    row = jnp.where(
        z == 0,
        layer(0),
        jnp.where(
            first & (z == 1),
            low[:lift],
            jnp.where((core == 1) & (z == 3), low[lift:], high),
        ),
    )
    column, row, labels = lax.optimization_barrier((column, row, labels))

    column_across = send(
        column,
        lambda xl, z, xh, y, core: (xl, z, 1, y, core),
        lambda xl, z, xh, y, core: xh == 0,
    )
    row_across = send(
        row,
        lambda xl, z, xh, y, core: (1, z, xh, y, core),
        lambda xl, z, xh, y, core: xl == 0,
    )
    pivot = spread(pivot, 2)
    labels = lax.all_to_all(labels, AXES, 0, 0, tiled=True)
    pivot = spread(pivot, 3)
    pivot = spread(pivot, 4)
    column = jnp.where(xh == 0, column, column_across)
    row = jnp.where(xl == 0, row, row_across)
    column, row, pivot, labels = lax.optimization_barrier((column, row, pivot, labels))

    def around(value, step):
        return send(
            value,
            lambda xl, z, xh, y, core: (xl, z, xh, partner(y, (core == 0) == (step == 0)), core),
        )

    def along(value, step):
        return send(
            value,
            lambda xl, z, xh, y, core: (xl, partner(z, (core == 0) == (step == 0)), xh, y, core),
        )

    row_a, column_a = along(row, 0), around(column, 0)
    row_b, column_b = along(row, 1), around(column, 1)
    other = swap(column)
    pivot = spread(pivot, 5)
    column_a, row_a = lax.optimization_barrier((column_a, row_a))
    row_c, column_c = along(row_a, 1), around(column_a, 1)
    pivots = (pivot, swap(pivot))
    other_a, other_b = swap(column_a), swap(column_b)
    other_c = swap(column_c)

    def order(k, core):
        one = jnp.where(core == 0, k ^ 1, 3 - k)
        two = jnp.where(core == 0, 3 - k, k ^ 1)
        return [k, one, two, 3 - (k ^ 1)]

    pieces = [column, other, column_a, column_b, other_a, other_b, column_c, other_c]
    mine = [4 * core + k for k in order(y, core)]
    theirs = [4 * (1 - core) + k for k in order(y, 1 - core)]
    numbers = [mine[0], theirs[0], mine[1], mine[2], theirs[1], theirs[2], mine[3], theirs[3]]
    return pieces, numbers, [row, row_a, row_b, row_c], order(z, core), pivots, labels


def halves(value):
    high = value.astype(jnp.bfloat16)
    low = (value - high.astype(jnp.float32)).astype(jnp.bfloat16)
    return high, low


def dot(left, right):
    return jnp.dot(left, right, preferred_element_type=jnp.float32)


def product(left, right):
    left_high, left_low = halves(left)
    right_high, right_low = halves(right)
    return dot(left_high, right_low) + dot(left_low, right_high) + dot(left_high, right_high)


def update_kernel(
    table_ref, owner_ref, front_ref, pivot_ref, other_ref, inverse_ref, *refs
):
    column_refs = refs[:8]
    row_refs = refs[8:12]
    updated_ref, outgoing_ref, mine_ref = refs[12:15]
    right, high, low, held, result, held_sem, whole_sem, block_sem = refs[15:]
    depth = inverse_ref.shape[1]
    step = pl.program_id(0)
    steps = pl.num_programs(0)
    slot = lax.rem(step, 2)
    tile = result.shape[1]
    edge = outgoing_ref.shape[1]
    down, across = tile // edge, result.shape[2] // edge

    def fetch(number, at):
        return pltpu.make_async_copy(column_refs[number], held.at[at], held_sem.at[at])

    def whole_copy(at, number):
        top = pl.multiple_of(table_ref[number] * tile, tile)
        return pltpu.make_async_copy(
            result.at[at], updated_ref.at[pl.ds(top, tile)], whole_sem.at[at]
        )

    def block_copies(at, number, act):
        for i in range(down):
            for j in range(across):
                owner = owner_ref[table_ref[number] * down + i, j]

                @pl.when(owner >= 0)
                def _():
                    act(
                        pltpu.make_async_copy(
                            result.at[at, pl.ds(i * edge, edge), pl.ds(j * edge, edge)],
                            outgoing_ref.at[jnp.maximum(owner, 0)],
                            block_sem.at[at],
                        )
                    )

    def finish(at, number):
        whole_copy(at, number).wait()
        block_copies(at, number, lambda copy: copy.wait())

    @pl.when(step == 0)
    def _():
        fetch(0, 0).start()
        lift = row_refs[0].shape[0]
        for k in range(4):
            top = pl.multiple_of(table_ref[8 + k] * lift, lift)
            right[pl.ds(top, lift)] = row_refs[k][...]
        first = table_ref[14] == 0
        pivot_one = jnp.where(first, pivot_ref[...], other_ref[...])
        pivot_two = jnp.where(first, other_ref[...], pivot_ref[...])
        one = right[:depth]
        two = right[depth:] - product(pivot_two, one)
        two = product(inverse_ref[0], two)
        high[depth:], low[depth:] = halves(two)
        one = one - product(pivot_one, two)
        high[:depth], low[:depth] = halves(one)

    for number in range(8):

        @pl.when(step == number)
        def _():
            if number < 7:
                fetch(number + 1, (number + 1) % 2).start()
            fetch(number, number % 2).wait()

    @pl.when(step >= 2)
    def _():
        finish(slot, step - 2)

    left = held[slot]
    left_high, left_low = halves(left)
    total = front_ref[...] - dot(left_high, low[...])
    total -= dot(left_low, high[...])
    total -= dot(left_high, high[...])
    result[slot] = total
    whole_copy(slot, step).start()
    block_copies(slot, step, lambda copy: copy.start())

    @pl.when(table_ref[step] == table_ref[12])
    def _():
        top = pl.multiple_of(table_ref[13] * edge, edge)
        mine_ref[...] = held[slot, pl.ds(top, edge)]

    @pl.when(step == steps - 1)
    def _():
        finish(1 - slot, step - 1)
        finish(slot, step)


def update(front, block_owner, pivots, inverses, pieces, layers, table, devices, edge):
    rows, columns = front.shape
    depth = inverses.shape[1]
    tile = pieces[0].shape[0]
    whole = lambda *shape: pl.BlockSpec(shape, lambda i, table: (0,) * len(shape))
    return pl.pallas_call(
        update_kernel,
        grid_spec=pltpu.PrefetchScalarGridSpec(
            num_scalar_prefetch=1,
            grid=(rows // tile,),
            in_specs=[
                pl.BlockSpec(memory_space=pltpu.SMEM),
                pl.BlockSpec((tile, columns), lambda i, table: (table[i], 0)),
                whole(depth, depth),
                whole(depth, depth),
                pl.BlockSpec((1, depth, depth), lambda i, table: (1, 0, 0)),
            ]
            + [pl.BlockSpec(memory_space=pl.ANY)] * 8
            + [whole(*layers[0].shape)] * 4,
            out_specs=[
                pl.BlockSpec(memory_space=pl.ANY),
                pl.BlockSpec(memory_space=pl.ANY),
                whole(edge, pieces[0].shape[1]),
            ],
            scratch_shapes=[
                pltpu.VMEM((2 * depth, columns), jnp.float32),
                pltpu.VMEM((2 * depth, columns), jnp.bfloat16),
                pltpu.VMEM((2 * depth, columns), jnp.bfloat16),
                pltpu.VMEM((2, tile, pieces[0].shape[1]), jnp.float32),
                pltpu.VMEM((2, tile, columns), jnp.float32),
                pltpu.SemaphoreType.DMA((2,)),
                pltpu.SemaphoreType.DMA((2,)),
                pltpu.SemaphoreType.DMA((2,)),
            ],
        ),
        out_shape=[
            jax.ShapeDtypeStruct((rows, columns), jnp.float32),
            jax.ShapeDtypeStruct((devices, edge, edge), jnp.float32),
            jax.ShapeDtypeStruct((edge, pieces[0].shape[1]), jnp.float32),
        ],
        compiler_params=pltpu.CompilerParams(vmem_limit_bytes=46 * MIB),
        cost_estimate=pl.CostEstimate(
            flops=16 * rows * columns * depth,
            bytes_accessed=40 * MIB,
            transcendentals=0,
        ),
        name="update",
    )(table, block_owner, front, *pivots, inverses, *pieces, *layers)


def add_kernel(slot_ref, parent_ref, arrived_ref, out_ref, sem):
    step = pl.program_id(0)
    count = arrived_ref.shape[0]

    @pl.when(step == 0)
    def _():
        copy = pltpu.make_async_copy(parent_ref, out_ref, sem)
        copy.start()
        copy.wait()

    for k in range(count):
        slot = slot_ref[step * count + k]

        @pl.when(slot >= 0)
        def _():
            at = jnp.maximum(slot, 0)
            out_ref[at] = out_ref[at] + arrived_ref[k]


def extend_add(slots, parent, arrived):
    count = 16
    held, edge, _ = parent.shape
    return pl.pallas_call(
        add_kernel,
        grid=(arrived.shape[0] // count,),
        in_specs=[
            pl.BlockSpec(memory_space=pltpu.SMEM),
            pl.BlockSpec(memory_space=pl.ANY),
            pl.BlockSpec((count, edge, edge), lambda i: (i, 0, 0)),
        ],
        out_specs=pl.BlockSpec((held, edge, edge), lambda i: (0, 0, 0)),
        out_shape=jax.ShapeDtypeStruct(parent.shape, jnp.float32),
        scratch_shapes=[pltpu.SemaphoreType.DMA],
        compiler_params=pltpu.CompilerParams(vmem_limit_bytes=32 * MIB),
        cost_estimate=pl.CostEstimate(flops=2 * MIB, bytes_accessed=14 * MIB, transcendentals=0),
        name="extend_add",
    )(slots, parent, arrived)


def exact(left, right):
    return jnp.dot(left, right, preferred_element_type=jnp.float32, precision=lax.Precision.HIGHEST)


def local(front, inverses, block_owner, block_slot, parent_in):
    width = inverses.shape[1]
    edge = parent_in.shape[1]
    devices = lax.axis_size("row") * lax.axis_size("col")
    col = lax.axis_index("col")

    columns = front[:, : 2 * width]

    def make_rows(front):
        return jnp.concatenate(
            [product_rows(inverses[0], front[:width]), front[width : 2 * width]], axis=0
        )

    owners = block_owner.reshape(-1)
    slots = block_slot.reshape(-1)
    named = owners[None, :] == jnp.arange(devices, dtype=jnp.int32)[:, None]
    labels = jnp.sum(jnp.where(named, slots[None, :] + 1, 0), axis=1).astype(jnp.float32)
    pieces, numbers, layers, heights, pivots, labels = exchange(
        front, columns, make_rows, labels.reshape(devices, 1, 1)
    )
    markers = labels.reshape(devices).astype(jnp.int32) - 1
    core = col % 2
    table = jnp.stack(numbers + heights + [col // 2, col % 2, core]).astype(jnp.int32)
    updated, outgoing, mine = update(
        front, block_owner, pivots, inverses, pieces, layers, table, devices, edge
    )
    arrived = lax.all_to_all(outgoing, AXES, 0, 0, tiled=True)

    mine_one, mine_two = mine[:, :width], mine[:, width:]
    corner = jnp.where(core == 0, pivots[0], pivots[1])
    mine_two = mine_two - exact(mine_one, corner)
    panels = jnp.concatenate([exact(mine_one, inverses[0]), exact(mine_two, inverses[1])], axis=1)
    parent_out = extend_add(markers, parent_in, arrived)
    return (updated, panels, parent_out)


def product_rows(left, right):
    return jnp.dot(left, right, preferred_element_type=jnp.float32, precision=lax.Precision.HIGH)


def solution(mesh):
    in_specs = (
        P("row", "col"),
        P(),
        P("row", "col"),
        P("row", "col"),
        P(("row", "col"), None, None),
    )
    out_specs = (P("row", "col"), P(("row", "col"), None), P(("row", "col"), None, None))
    return jax.shard_map(local, mesh=mesh, in_specs=in_specs, out_specs=out_specs, check_vma=False)
```

```python
import jax
import jax.numpy as jnp
from jax import lax
from jax.experimental import pallas as pl
from jax.experimental.pallas import tpu as pltpu
from jax.sharding import PartitionSpec as P

AXES = ("row", "col")
MIB = 1024 * 1024


def device(xl, z, xh, y, core):
    return (xl * 4 + z) * 16 + xh * 8 + y * 2 + core


def pairs(move, keep=lambda *place: True):
    listed = []
    for xl in range(2):
        for z in range(4):
            for xh in range(2):
                for y in range(4):
                    for core in range(2):
                        place = (xl, z, xh, y, core)
                        if keep(*place):
                            listed.append((device(*place), device(*move(*place))))
    return listed


def send(value, move, keep=lambda *place: True):
    return lax.ppermute(value, AXES, pairs(move, keep))


def place():
    row = lax.axis_index("row")
    col = lax.axis_index("col")
    return row // 4, row % 4, col // 8, (col // 2) % 4, col % 2


def partner(k, first):
    return k ^ 1 if first else 3 - k


def moved(spot, step):
    xl, z, xh, y = spot
    if step[0] == "z":
        return (xl, partner(z, step == "z0"), xh, y)
    if step[0] == "y":
        return (xl, z, xh, partner(y, step == "y0"))
    return (1 - xl, z, xh, y) if step == "xl" else (xl, z, 1 - xh, y)


def doubling():
    orders = (("xl", "xh", "z0", "z1", "y0", "y1"), ("xh", "xl", "y0", "y1", "z0", "z1"))
    having = [{(0, 0, 0, 0)}, {(0, 0, 0, 0)}]
    rounds = []
    for number in range(6):
        listed = []
        for core in range(2):
            new = {moved(spot, orders[core][number]): spot for spot in sorted(having[core])}
            for to, start in new.items():
                listed.append((device(*start, core), device(*to, core)))
            having[core] = having[core] | set(new)
        rounds.append(listed)
    return rounds


def exchange(front, columns, make_rows, labels):
    xl, z, xh, y, core = place()
    first = core == 0
    edge = columns.shape[0] // 8
    lift = columns.shape[1] // 4
    part = lambda k, count=1: columns[k * edge : (k + count) * edge]
    layer = lambda k, count=1: rows[k * lift : (k + count) * lift]
    rounds = doubling()
    corner = ((xl == 0) & (z == 0)) & ((xh == 0) & (y == 0))

    def swap(value):
        return send(value, lambda xl, z, xh, y, core: (xl, z, xh, y, 1 - core))

    def spread(value, number):
        return value + lax.ppermute(value, AXES, rounds[number])

    source = lambda xl, z, xh, y, core: xh == 0 and y == 0 and core == 0

    half = columns.shape[1] // 2
    beside = lax.ppermute(columns[half : 2 * half, :half], AXES, [(0, 1)])

    one = send(part(1, 2), lambda xl, z, xh, y, core: (xl, z, xh, 1, 0), source)
    two = send(part(6, 2), lambda xl, z, xh, y, core: (xl, z, xh, 3, 1), source)
    beside, front = lax.optimization_barrier((beside, front))
    rows = make_rows(front)
    low = send(
        jnp.where(first, layer(1, 2), layer(2, 2)),
        lambda xl, z, xh, y, core: (xl, partner(z, core == 0), xh, y, core),
        lambda xl, z, xh, y, core: xl == 0 and z == 0,
    )
    pivot = jnp.where(corner & first, rows[:half, half:], beside)
    pivot = spread(pivot, 0)
    one, two, low, pivot, columns, rows = lax.optimization_barrier(
        (one, two, low, pivot, columns, rows)
    )

    three = send(
        jnp.where(y == 0, part(3), one[edge:]),
        lambda xl, z, xh, y, core: (xl, z, xh, 3 - y, 0),
        lambda xl, z, xh, y, core: xh == 0 and core == 0 and y in (0, 1),
    )
    four = send(
        jnp.where(y == 0, part(5), two[:edge]),
        lambda xl, z, xh, y, core: (xl, z, xh, y ^ 1, 1),
        lambda xl, z, xh, y, core: xh == 0 and ((core == 0 and y == 0) or (core == 1 and y == 3)),
    )
    high = send(
        jnp.where(
            z == 0,
            jnp.where(first, layer(3), layer(1)),
            jnp.where(first, low[lift:], low[:lift]),
        ),
        lambda xl, z, xh, y, core: (xl, partner(z, core == 1), xh, y, core),
        lambda xl, z, xh, y, core: xl == 0 and z in ((0, 1) if core == 0 else (0, 3)),
    )
    five = send(part(4), lambda xl, z, xh, y, core: (xl, z, xh, y, 1), source)
    pivot = spread(pivot, 1)
    column = jnp.where(
        first,
        jnp.where(y == 0, part(0), jnp.where(y == 1, one[:edge], three)),
        jnp.where(y == 0, five, jnp.where(y == 3, two[edge:], four)),
    )
    row = jnp.where(
        z == 0,
        layer(0),
        jnp.where(
            first & (z == 1),
            low[:lift],
            jnp.where((core == 1) & (z == 3), low[lift:], high),
        ),
    )
    column, row, pivot, labels = lax.optimization_barrier((column, row, pivot, labels))

    column_across = send(
        column,
        lambda xl, z, xh, y, core: (xl, z, 1, y, core),
        lambda xl, z, xh, y, core: xh == 0,
    )
    row_across = send(
        row,
        lambda xl, z, xh, y, core: (1, z, xh, y, core),
        lambda xl, z, xh, y, core: xl == 0,
    )
    pivot = spread(pivot, 2)
    labels = lax.all_to_all(labels, AXES, 0, 0, tiled=True)
    pivot = spread(pivot, 3)
    pivot = spread(pivot, 4)
    column = jnp.where(xh == 0, column, column_across)
    row = jnp.where(xl == 0, row, row_across)
    column, row, labels = lax.optimization_barrier((column, row, labels))

    def around(value, step):
        return send(
            value,
            lambda xl, z, xh, y, core: (xl, z, xh, partner(y, (core == 0) == (step == 0)), core),
        )

    def along(value, step):
        return send(
            value,
            lambda xl, z, xh, y, core: (xl, partner(z, (core == 0) == (step == 0)), xh, y, core),
        )

    row_a, column_a = along(row, 0), around(column, 0)
    row_b, column_b = along(row, 1), around(column, 1)
    other = swap(column)
    pivot = spread(pivot, 5)
    column_a, row_a = lax.optimization_barrier((column_a, row_a))
    row_c, column_c = along(row_a, 1), around(column_a, 1)
    pivots = (pivot, swap(pivot))
    other_a, other_b = swap(column_a), swap(column_b)
    other_c = swap(column_c)

    def order(k, core):
        one = jnp.where(core == 0, k ^ 1, 3 - k)
        two = jnp.where(core == 0, 3 - k, k ^ 1)
        return [k, one, two, 3 - (k ^ 1)]

    pieces = [column, other, column_a, column_b, other_a, other_b, column_c, other_c]
    mine = [4 * core + k for k in order(y, core)]
    theirs = [4 * (1 - core) + k for k in order(y, 1 - core)]
    numbers = [mine[0], theirs[0], mine[1], mine[2], theirs[1], theirs[2], mine[3], theirs[3]]
    return pieces, numbers, [row, row_a, row_b, row_c], order(z, core), pivots, labels


def halves(value):
    high = value.astype(jnp.bfloat16)
    low = (value - high.astype(jnp.float32)).astype(jnp.bfloat16)
    return high, low


def dot(left, right):
    return jnp.dot(left, right, preferred_element_type=jnp.float32)


def product(left, right):
    left_high, left_low = halves(left)
    right_high, right_low = halves(right)
    return dot(left_high, right_low) + dot(left_low, right_high) + dot(left_high, right_high)


def update_kernel(
    table_ref, owner_ref, front_ref, pivot_ref, other_ref, inverse_ref, *refs
):
    column_refs = refs[:8]
    row_refs = refs[8:12]
    updated_ref, outgoing_ref, mine_ref = refs[12:15]
    right, high, low, held, result, held_sem, whole_sem, block_sem = refs[15:]
    depth = inverse_ref.shape[1]
    step = pl.program_id(0)
    steps = pl.num_programs(0)
    slot = lax.rem(step, 2)
    tile = result.shape[1]
    edge = outgoing_ref.shape[1]
    down, across = tile // edge, result.shape[2] // edge

    def fetch(number, at):
        return pltpu.make_async_copy(column_refs[number], held.at[at], held_sem.at[at])

    def whole_copy(at, number):
        top = pl.multiple_of(table_ref[number] * tile, tile)
        return pltpu.make_async_copy(
            result.at[at], updated_ref.at[pl.ds(top, tile)], whole_sem.at[at]
        )

    def block_copies(at, number, act):
        for i in range(down):
            for j in range(across):
                owner = owner_ref[table_ref[number] * down + i, j]

                @pl.when(owner >= 0)
                def _():
                    act(
                        pltpu.make_async_copy(
                            result.at[at, pl.ds(i * edge, edge), pl.ds(j * edge, edge)],
                            outgoing_ref.at[jnp.maximum(owner, 0)],
                            block_sem.at[at],
                        )
                    )

    def finish(at, number):
        whole_copy(at, number).wait()
        block_copies(at, number, lambda copy: copy.wait())

    @pl.when(step == 0)
    def _():
        fetch(0, 0).start()
        lift = row_refs[0].shape[0]
        for k in range(4):
            top = pl.multiple_of(table_ref[8 + k] * lift, lift)
            right[pl.ds(top, lift)] = row_refs[k][...]
        first = table_ref[14] == 0
        pivot_one = jnp.where(first, pivot_ref[...], other_ref[...])
        pivot_two = jnp.where(first, other_ref[...], pivot_ref[...])
        one = right[:depth]
        two = right[depth:] - product(pivot_two, one)
        two = product(inverse_ref[0], two)
        high[depth:], low[depth:] = halves(two)
        one = one - product(pivot_one, two)
        high[:depth], low[:depth] = halves(one)

    for number in range(8):

        @pl.when(step == number)
        def _():
            if number < 7:
                fetch(number + 1, (number + 1) % 2).start()
            fetch(number, number % 2).wait()

    @pl.when(step >= 2)
    def _():
        finish(slot, step - 2)

    left = held[slot]
    left_high, left_low = halves(left)
    total = front_ref[...] - dot(left_high, low[...])
    total -= dot(left_low, high[...])
    total -= dot(left_high, high[...])
    result[slot] = total
    whole_copy(slot, step).start()
    block_copies(slot, step, lambda copy: copy.start())

    @pl.when(table_ref[step] == table_ref[12])
    def _():
        top = pl.multiple_of(table_ref[13] * edge, edge)
        mine_ref[...] = held[slot, pl.ds(top, edge)]

    @pl.when(step == steps - 1)
    def _():
        finish(1 - slot, step - 1)
        finish(slot, step)


def update(front, block_owner, pivots, inverses, pieces, layers, table, devices, edge):
    rows, columns = front.shape
    depth = inverses.shape[1]
    tile = pieces[0].shape[0]
    whole = lambda *shape: pl.BlockSpec(shape, lambda i, table: (0,) * len(shape))
    return pl.pallas_call(
        update_kernel,
        grid_spec=pltpu.PrefetchScalarGridSpec(
            num_scalar_prefetch=1,
            grid=(rows // tile,),
            in_specs=[
                pl.BlockSpec(memory_space=pltpu.SMEM),
                pl.BlockSpec((tile, columns), lambda i, table: (table[i], 0)),
                whole(depth, depth),
                whole(depth, depth),
                pl.BlockSpec((1, depth, depth), lambda i, table: (1, 0, 0)),
            ]
            + [pl.BlockSpec(memory_space=pl.ANY)] * 8
            + [whole(*layers[0].shape)] * 4,
            out_specs=[
                pl.BlockSpec(memory_space=pl.ANY),
                pl.BlockSpec(memory_space=pl.ANY),
                whole(edge, pieces[0].shape[1]),
            ],
            scratch_shapes=[
                pltpu.VMEM((2 * depth, columns), jnp.float32),
                pltpu.VMEM((2 * depth, columns), jnp.bfloat16),
                pltpu.VMEM((2 * depth, columns), jnp.bfloat16),
                pltpu.VMEM((2, tile, pieces[0].shape[1]), jnp.float32),
                pltpu.VMEM((2, tile, columns), jnp.float32),
                pltpu.SemaphoreType.DMA((2,)),
                pltpu.SemaphoreType.DMA((2,)),
                pltpu.SemaphoreType.DMA((2,)),
            ],
        ),
        out_shape=[
            jax.ShapeDtypeStruct((rows, columns), jnp.float32),
            jax.ShapeDtypeStruct((devices, edge, edge), jnp.float32),
            jax.ShapeDtypeStruct((edge, pieces[0].shape[1]), jnp.float32),
        ],
        compiler_params=pltpu.CompilerParams(vmem_limit_bytes=46 * MIB),
        cost_estimate=pl.CostEstimate(
            flops=16 * rows * columns * depth,
            bytes_accessed=40 * MIB,
            transcendentals=0,
        ),
        name="update",
    )(table, block_owner, front, *pivots, inverses, *pieces, *layers)


def add_kernel(slot_ref, parent_ref, arrived_ref, out_ref, sem):
    step = pl.program_id(0)
    count = arrived_ref.shape[0]

    @pl.when(step == 0)
    def _():
        copy = pltpu.make_async_copy(parent_ref, out_ref, sem)
        copy.start()
        copy.wait()

    for k in range(count):
        slot = slot_ref[step * count + k]

        @pl.when(slot >= 0)
        def _():
            at = jnp.maximum(slot, 0)
            out_ref[at] = out_ref[at] + arrived_ref[k]


def extend_add(slots, parent, arrived):
    count = 16
    held, edge, _ = parent.shape
    return pl.pallas_call(
        add_kernel,
        grid=(arrived.shape[0] // count,),
        in_specs=[
            pl.BlockSpec(memory_space=pltpu.SMEM),
            pl.BlockSpec(memory_space=pl.ANY),
            pl.BlockSpec((count, edge, edge), lambda i: (i, 0, 0)),
        ],
        out_specs=pl.BlockSpec((held, edge, edge), lambda i: (0, 0, 0)),
        out_shape=jax.ShapeDtypeStruct(parent.shape, jnp.float32),
        scratch_shapes=[pltpu.SemaphoreType.DMA],
        compiler_params=pltpu.CompilerParams(vmem_limit_bytes=32 * MIB),
        cost_estimate=pl.CostEstimate(flops=2 * MIB, bytes_accessed=14 * MIB, transcendentals=0),
        name="extend_add",
    )(slots, parent, arrived)


def exact(left, right):
    return jnp.dot(left, right, preferred_element_type=jnp.float32, precision=lax.Precision.HIGHEST)


def local(front, inverses, block_owner, block_slot, parent_in):
    width = inverses.shape[1]
    edge = parent_in.shape[1]
    devices = lax.axis_size("row") * lax.axis_size("col")
    col = lax.axis_index("col")

    columns = front[:, : 2 * width]

    def make_rows(front):
        return jnp.concatenate(
            [product_rows(inverses[0], front[:width]), front[width : 2 * width]], axis=0
        )

    owners = block_owner.reshape(-1)
    slots = block_slot.reshape(-1)
    named = owners[None, :] == jnp.arange(devices, dtype=jnp.int32)[:, None]
    labels = jnp.sum(jnp.where(named, slots[None, :] + 1, 0), axis=1).astype(jnp.float32)
    pieces, numbers, layers, heights, pivots, labels = exchange(
        front, columns, make_rows, labels.reshape(devices, 1, 1)
    )
    markers = labels.reshape(devices).astype(jnp.int32) - 1
    core = col % 2
    table = jnp.stack(numbers + heights + [col // 2, col % 2, core]).astype(jnp.int32)
    updated, outgoing, mine = update(
        front, block_owner, pivots, inverses, pieces, layers, table, devices, edge
    )
    arrived = lax.all_to_all(outgoing, AXES, 0, 0, tiled=True)

    mine_one, mine_two = mine[:, :width], mine[:, width:]
    corner = jnp.where(core == 0, pivots[0], pivots[1])
    mine_two = mine_two - exact(mine_one, corner)
    panels = jnp.concatenate([exact(mine_one, inverses[0]), exact(mine_two, inverses[1])], axis=1)
    parent_out = extend_add(markers, parent_in, arrived)
    return (updated, panels, parent_out)


def product_rows(left, right):
    return jnp.dot(left, right, preferred_element_type=jnp.float32, precision=lax.Precision.HIGH)


def solution(mesh):
    in_specs = (
        P("row", "col"),
        P(),
        P("row", "col"),
        P("row", "col"),
        P(("row", "col"), None, None),
    )
    out_specs = (P("row", "col"), P(("row", "col"), None), P(("row", "col"), None, None))
    return jax.shard_map(local, mesh=mesh, in_specs=in_specs, out_specs=out_specs, check_vma=False)
```
